32 devices in a mesh: fsdp: 16 (over z, y, core), tp: 2 (over x).
Axes of the slice: x: 2, y: 2, z: 4, core: 2. Of those that a mesh axis runs over, the one named last changes fastest.
Arguments:
- tokens: bfloat16 [16384, 1024], P(('fsdp', 'tp')), may hold values from -6 to 6
- seq_lens: int32 [16, 4], P('fsdp'), may hold values from 1 to 512, 1024 in all within a row
- routes: int32 [16384, 8], P('fsdp'), may hold values from 0 to 15, all different within a row; in each aligned block of 1024 rows (0 to 1023, 1024 to 2047, ...) at most 768 rows name the same one
- route_gates: float32 [16384, 8], P('fsdp'), may hold values from 0.06 to 0.19
- query_weight: bfloat16 [1024, 1024], P('fsdp', 'tp'), may hold values from -0.25 to 0.25
- key_matrix: bfloat16 [1024, 512], P('fsdp', 'tp'), may hold values from -0.25 to 0.25
- value_matrix: bfloat16 [1024, 512], P('fsdp', 'tp'), may hold values from -0.1875 to 0.1875
- out_weight: bfloat16 [1024, 1024], P('fsdp', 'tp'), may hold values from -6 to 6
- norm_gains: bfloat16 [2, 1024], P(None, 'fsdp'), may hold values from 0.5 to 1.5
- gate_weight: bfloat16 [16, 1024, 512], P(None, 'fsdp', 'tp'), may hold values from -0.1875 to 0.1875
- up_weight: bfloat16 [16, 1024, 512], P(None, 'fsdp', 'tp'), may hold values from -0.1875 to 0.1875
- down_weight: bfloat16 [16, 1024, 512], P(None, 'fsdp', 'tp'), may hold values from -6 to 6
- cotangent: bfloat16 [16384, 1024], P(('fsdp', 'tp')), may hold values from -6 to 6
Outputs:
- layer_out: bfloat16 [16384, 1024], P(('fsdp', 'tp'))
- grad_tokens: bfloat16 [16384, 1024], P(('fsdp', 'tp'))
- grad_query: float32 [1024, 1024], P('fsdp', 'tp')
- grad_key: float32 [1024, 512], P('fsdp', 'tp')
- grad_value: float32 [1024, 512], P('fsdp', 'tp')
- grad_out_weight: float32 [1024, 1024], P('fsdp', 'tp')
- grad_gains: float32 [2, 1024], P(None, 'fsdp')
- grad_gate: float32 [16, 1024, 512], P(None, 'fsdp', 'tp')
- grad_up: float32 [16, 1024, 512], P(None, 'fsdp', 'tp')
- grad_down: float32 [16, 1024, 512], P(None, 'fsdp', 'tp')
The draws below stay inside these ranges and needn't reach their ends.
Inputs may be any that keep to these rules, and one draw needn't show every extreme that they name: Within the 1024 routes rows of one group (aligned blocks) no expert is named by more than 768 rows, a bound that some block reaches. `seq_lens`: each row sums to 1024; its largest length is 512.
All inputs are finite; a program needn't handle non-finite values.
Results may differ from the reference program's by a relative error of at most 0.018.
Values may be sent and summed in bfloat16 or wider, within the bound.
No kernel may reach another device: no remote copies, remote signals or barrier semaphores. Data moves between devices by JAX's collectives and lax.ppermute only.
A program may use at most 384 MiB of HBM per device.

```python
import math
import jax
import jax.numpy as jnp
import numpy as np
from jax import lax

MODEL_DIM = 1024
NQH = 16
KEY_VALUE_HEADS = 8
HEAD_DIM = 64
FF = 512
EXPERTS = 16
TOP = 8
TOK_DEV = 1024
NSEQ = 4
MAXLEN = 512
CAP = 768
GROUPS = 16
TOKENS = 16384


def steps_of(key, dims, shards, low, top_value):
    level = 1.0
    for axis_at, parts in shards:
        heights = jax.random.uniform(jax.random.fold_in(jax.random.fold_in(key, 6), axis_at), (parts,), jnp.float32, low / len(shards), top_value / len(shards))
        level = level * jnp.repeat(jnp.exp(heights), dims[axis_at] // parts).reshape((-1,) + (1,) * (len(dims) - 1 - axis_at))
    return level


def length_profile(amount, total, bound, slope):
    weights = [(1 << 20) // math.isqrt(grade ** slope) + 1 for grade in range(2, amount + 1)]
    surplus, holding = total - bound - (amount - 1), [1] * (amount - 1)
    while surplus > 0:
        candidates = [i for i in range(amount - 1) if holding[i] < bound]
        pool, left = sum([weights[i] for i in candidates]), surplus
        for i in candidates:
            addition = min(bound - holding[i], max(1, left * weights[i] // pool), surplus)
            holding[i] = holding[i] + addition
            surplus = surplus - addition
    return np.array([bound] + holding)


def uneven(stream_key, number_of, total, bound, lean):
    if number_of == 2:
        one = jax.random.randint(stream_key, (), max(1, total - bound), min(bound, total - 1) + 1)
        return jnp.stack([one, total - one])
    sizes = jnp.asarray(length_profile(number_of, total, bound, lean), jnp.int32)
    couples = (number_of - 1) // 2
    giver, receiver = sizes[1:1 + 2 * couples:2], sizes[2:2 + 2 * couples:2]
    margin = jnp.minimum(giver - 1, bound - receiver)
    passed = jax.random.randint(jax.random.fold_in(stream_key, 1), (couples,), 0, 1 << 20) % (margin + 1)
    sizes = sizes.at[1:1 + 2 * couples:2].set(giver - passed).at[2:2 + 2 * couples:2].set(receiver + passed)
    return sizes[jax.random.permutation(jax.random.fold_in(stream_key, 2), number_of)]


def deal_out(own_key, own, number, rows, amount, top, limit, skew):
    ranking = jax.random.permutation(own_key, amount)
    heavy_load, common = portions_of(amount, rows * top, limit, skew, True), portions_of(amount, rows * top, limit, skew, False)
    places = jnp.arange(amount)

    def named(tallies, rotation):
        used = int((tallies > 0).sum())
        fixed = max(1, used // 4)
        shifted = fixed + (places - fixed + rotation * (used - fixed)) % max(1, amount - fixed)
        return jnp.zeros((amount,), jnp.int32).at[ranking[jnp.where(places < fixed, places, shifted)]].set(jnp.asarray(tallies, jnp.int32))

    tallies = jnp.where(number % 4 == 0, named(heavy_load, number // 4), named(common, number - number // 4 - 1))
    mixed = jax.random.permutation(jax.random.fold_in(own, 3), amount)
    source_of, taker = mixed[0:amount // 2 * 2:2], mixed[1:amount // 2 * 2:2]
    slack = jnp.minimum(tallies[source_of] - 1, limit - tallies[taker]) // 2
    slack = jnp.where((source_of == ranking[0]) | (taker == ranking[0]) | (tallies[taker] == 0), 0, jnp.maximum(slack, 0))
    shifted = jax.random.randint(jax.random.fold_in(own, 4), (amount // 2,), 0, 1 << 20) % (slack + 1)
    tallies = tallies.at[source_of].add(-shifted).at[taker].add(shifted)
    labels = jnp.searchsorted(jnp.cumsum(tallies), jnp.arange(rows * top), side="right").astype(jnp.int32)
    listing = labels.reshape(top, rows).T
    listing = listing[jax.random.permutation(jax.random.fold_in(own, 1), rows)]
    rotation = jax.random.randint(jax.random.fold_in(own, 2), (rows, 1), 0, top)
    return jnp.take_along_axis(listing, (jnp.arange(top)[None, :] + rotation) % top, axis=1)


def portions_of(amount, total, bound, slope, full):
    weights = [(1 << 20) // math.isqrt(standing ** slope) + 1 for standing in range(1, amount + 1)]
    largest = bound if full else min(bound, max(-(-total // amount), total * weights[0] // sum(weights)))
    least = 1 if total - largest >= amount - 1 else 0
    holding, rest = [largest] + [least] * (amount - 1), total - largest - least * (amount - 1)
    while rest > 0:
        candidates = [i for i in range(1, amount) if holding[i] < largest] or [i for i in range(1, amount) if holding[i] < bound]
        whole, remaining = sum([weights[i] for i in candidates]), rest
        for i in candidates:
            more = min(bound - holding[i], max(1, remaining * weights[i] // whole), rest)
            holding[i] = holding[i] + more
            rest = rest - more
    return np.array(holding)


def noise(rng, extent, spread, most, shards=(), kind=jnp.bfloat16):
    array = spread * jax.random.normal(rng, extent, jnp.float32)
    if shards:
        array = array * steps_of(rng, extent, shards, -0.22, 0.18)
    return jnp.clip(array, -most, most).astype(kind)


def setup_inputs(seed: int = 0) -> dict:
    keys = jax.random.split(jax.random.key(seed), 14)
    tokens = noise(keys[0], (TOKENS, MODEL_DIM), 1.0, 6.0, ((0, 32),))
    seq_lens = jax.vmap(lambda own: uneven(own, NSEQ, TOK_DEV, MAXLEN, 2))(jax.random.split(keys[1], GROUPS)).reshape((GROUPS, NSEQ)).astype(jnp.int32)
    routes_keys = jax.random.split(jax.random.fold_in(keys[2], 1), TOKENS // TOK_DEV)
    routes_turns = jax.random.permutation(jax.random.fold_in(keys[2], 3), TOKENS // TOK_DEV)
    routes = jax.vmap(lambda own, number: deal_out(jax.random.fold_in(keys[2], 2), own, number, TOK_DEV, EXPERTS, TOP, CAP, 1))(routes_keys, routes_turns).reshape((TOKENS, TOP))
    route_gates = jnp.clip(0.06 + 0.13 * jax.random.uniform(keys[3], (TOKENS, TOP), jnp.float32) ** steps_of(keys[3], (TOKENS, TOP), ((0, 16),), -0.2, 0.2), 0.06, 0.19)
    query_weight = noise(keys[4], (MODEL_DIM, NQH * HEAD_DIM), (MODEL_DIM // 2) ** -0.5, 0.25, ((0, 16), (1, 2)))
    key_matrix = noise(keys[5], (MODEL_DIM, KEY_VALUE_HEADS * HEAD_DIM), (MODEL_DIM // 2) ** -0.5, 0.25, ((0, 16), (1, 2)))
    value_matrix = noise(keys[6], (MODEL_DIM, KEY_VALUE_HEADS * HEAD_DIM), MODEL_DIM ** -0.5, 0.1875, ((0, 16), (1, 2)))
    out_weight = noise(keys[7], (MODEL_DIM, NQH * HEAD_DIM), 1 ** -0.5, 6.0, ((0, 16), (1, 2)))
    norm_gains = jnp.clip(1.0 + 0.1 * jax.random.normal(keys[8], (2, MODEL_DIM), jnp.float32), 0.5, 1.5).astype(jnp.bfloat16)
    gate_weight = noise(keys[9], (EXPERTS, MODEL_DIM, FF), MODEL_DIM ** -0.5, 0.1875, ((1, 16), (2, 2)))
    up_weight = noise(keys[10], (EXPERTS, MODEL_DIM, FF), MODEL_DIM ** -0.5, 0.1875, ((1, 16), (2, 2)))
    down_weight = noise(keys[11], (EXPERTS, MODEL_DIM, FF), 1 ** -0.5, 6.0, ((1, 16), (2, 2)))
    cotangent = noise(keys[12], (TOKENS, MODEL_DIM), 1.0, 6.0, ((0, 32),))
    return {"tokens": tokens, "seq_lens": seq_lens, "routes": routes, "route_gates": route_gates, "query_weight": query_weight, "key_matrix": key_matrix, "value_matrix": value_matrix, "out_weight": out_weight, "norm_gains": norm_gains, "gate_weight": gate_weight, "up_weight": up_weight, "down_weight": down_weight, "cotangent": cotangent}


EPSILON = 1e-06
BRANCH_SCALE = 0.22
ROPE_BASE = 10000.0
HIGHEST_PRECISION = lax.Precision.HIGHEST

@jax.custom_vjp
def low(v):
    return lax.optimization_barrier(v.astype(jnp.bfloat16)).astype(jnp.float32)

@jax.custom_vjp
def low_back(v):
    return v

def low_keep(v):
    return (low(v), None)

def low_pass(kept, grad):
    return (grad,)

def back_keep(v):
    return (v, None)

def back_low(kept, grad):
    return (low(grad),)
low.defvjp(low_keep, low_pass)
low_back.defvjp(back_keep, back_low)

def seq_layout(lengths, row_total):
    places = jnp.arange(row_total, dtype=jnp.int32)
    ends = jnp.cumsum(lengths).astype(jnp.int32)
    starts = ends - lengths
    segment = lax.optimization_barrier(jnp.sum((places[:, None] >= ends[None, :]).astype(jnp.int32), axis=1))
    chosen = segment[:, None] == jnp.arange(lengths.shape[0], dtype=jnp.int32)[None, :]
    opening = lax.optimization_barrier(jnp.sum(jnp.where(chosen, starts[None, :], 0), axis=1)).astype(jnp.int32)
    return (segment, places - opening)

def rotary_tables(position, head_size):
    halfway = head_size // 2
    ladder = jnp.arange(halfway, dtype=jnp.float32)
    inverse = jnp.exp(ladder * (-2.0 * jnp.log(ROPE_BASE) / head_size))
    angles = position.astype(jnp.float32)[:, None] * inverse[None, :]
    return (jnp.cos(angles), jnp.sin(angles))

def rotate(head_rows, cos_table, sine_table):
    halfway = head_rows.shape[-1] // 2
    first_half = head_rows[..., :halfway]
    second_half = head_rows[..., halfway:]
    cos_rows = cos_table[:, None, :]
    sine_rows = sine_table[:, None, :]
    return jnp.concatenate([first_half * cos_rows - second_half * sine_rows, second_half * cos_rows + first_half * sine_rows], axis=-1)

def route_slots(routes, experts, capacity):
    row_total, chosen = routes.shape
    flat_ids = routes.reshape(-1)
    onehot = (flat_ids[:, None] == jnp.arange(experts, dtype=jnp.int32)[None, :]).astype(jnp.int32)
    earlier = jnp.cumsum(onehot, axis=0) - onehot
    slot_place = lax.optimization_barrier(jnp.sum(earlier * onehot, axis=1)).astype(jnp.int32)
    slot_index = flat_ids * capacity + slot_place
    source = jnp.full((experts * capacity,), row_total * chosen, jnp.int32)
    source = source.at[slot_index].set(jnp.arange(row_total * chosen, dtype=jnp.int32))
    return (slot_index.reshape(row_total, chosen), source)

def attend(query_rows, key_rows, value_rows, segment, score_scale):
    row_total = query_rows.shape[0]
    block_rows = min(512, row_total)
    blocks = row_total // block_rows
    places = jnp.arange(row_total, dtype=jnp.int32)

    def one_block(query_blk, seg_blk, place_blk, key_all, value_all):
        scores = jnp.einsum('qjgd,kjd->jgqk', query_blk, key_all, precision=HIGHEST_PRECISION) * score_scale
        scores = low_back(scores)
        allowed = (seg_blk[:, None] == segment[None, :]) & (place_blk[:, None] >= places[None, :])
        scores = jnp.where(allowed[None, None], scores, -1e+30)
        row_peak = lax.optimization_barrier(jnp.max(scores, axis=-1, keepdims=True))
        weights = jnp.exp(scores - row_peak)
        prob_rows = weights / lax.optimization_barrier(jnp.sum(weights, axis=-1, keepdims=True))
        return jnp.einsum('jgqk,kjd->qjgd', low(prob_rows), value_all, precision=HIGHEST_PRECISION)
    checked_block = jax.checkpoint(one_block)
    outputs = lax.map(lambda block_item: checked_block(block_item[0], block_item[1], block_item[2], key_rows, value_rows), (query_rows.reshape((blocks, block_rows) + query_rows.shape[1:]), segment.reshape(blocks, block_rows), places.reshape(blocks, block_rows)))
    return outputs.reshape(query_rows.shape)

def layer(inputs, segment, position, routes, route_gates, query_weight, key_matrix, value_matrix, out_weight, norm_gains, gate_weight, up_weight, down_weight):
    row_total = inputs.shape[0]
    model_width = inputs.shape[1]
    kv_heads = key_matrix.shape[1] // HEAD_DIM
    group_size = query_weight.shape[1] // key_matrix.shape[1]
    scale_one = lax.rsqrt(lax.optimization_barrier(jnp.mean(inputs * inputs, axis=1, keepdims=True)) + EPSILON)
    normed_one = low(inputs * scale_one * norm_gains[0])
    cos_table, sine_table = rotary_tables(position, HEAD_DIM)
    query_raw = low_back(jnp.dot(normed_one, query_weight, precision=HIGHEST_PRECISION)).reshape(row_total, kv_heads * group_size, HEAD_DIM)
    query_rows = low(rotate(query_raw, cos_table, sine_table)).reshape(row_total, kv_heads, group_size, HEAD_DIM)
    key_raw = low_back(jnp.dot(normed_one, key_matrix, precision=HIGHEST_PRECISION)).reshape(row_total, kv_heads, HEAD_DIM)
    key_rows = low(rotate(key_raw, cos_table, sine_table))
    value_rows = low(low_back(jnp.dot(normed_one, value_matrix, precision=HIGHEST_PRECISION))).reshape(row_total, kv_heads, HEAD_DIM)
    attended = attend(query_rows, key_rows, value_rows, segment, HEAD_DIM ** (-0.5)).reshape(row_total, kv_heads * group_size * HEAD_DIM)
    attended = low(low_back(attended))
    attn_out = low_back(jnp.dot(attended, out_weight.T, precision=HIGHEST_PRECISION))
    middle = inputs + BRANCH_SCALE * attn_out
    scale_two = lax.rsqrt(lax.optimization_barrier(jnp.mean(middle * middle, axis=1, keepdims=True)) + EPSILON)
    normed_two = low(middle * scale_two * norm_gains[1])
    slot_index, source = route_slots(routes, EXPERTS, CAP)
    padded = jnp.concatenate([normed_two, jnp.zeros((1, model_width), normed_two.dtype)], axis=0)
    expert_rows = padded[source // routes.shape[1]].reshape(EXPERTS, CAP, model_width)
    gate_pre = low_back(jnp.einsum('ecd,edf->ecf', expert_rows, gate_weight, precision=HIGHEST_PRECISION))
    up_pre = low_back(jnp.einsum('ecd,edf->ecf', expert_rows, up_weight, precision=HIGHEST_PRECISION))
    hidden = low(jax.nn.silu(gate_pre) * up_pre)
    expert_out = low_back(jnp.einsum('ecf,edf->ecd', hidden, down_weight, precision=HIGHEST_PRECISION)).reshape(EXPERTS * CAP, model_width)
    combined = lax.optimization_barrier(jnp.sum(route_gates[:, :, None] * expert_out[slot_index], axis=1))
    return middle + BRANCH_SCALE * combined

def reference(tokens, seq_lens, routes, route_gates, query_weight, key_matrix, value_matrix, out_weight, norm_gains, gate_weight, up_weight, down_weight, cotangent):
    groups = seq_lens.shape[0]
    chosen = routes.shape[1]
    model_width = tokens.shape[1]
    gate_values = route_gates.astype(jnp.float32).reshape(groups, -1, chosen)
    route_groups = routes.reshape(groups, -1, chosen)

    def forward(inputs, query_w, key_w, value_w, out_w, gains, gate_w, up_w, down_w):
        checked_layer = jax.checkpoint(layer)

        def group_step(running, block_item):
            part_in, lengths, part_routes, part_gates = block_item
            segment, position = seq_layout(lengths, part_in.shape[0])
            return (running, checked_layer(part_in, segment, position, part_routes, part_gates, query_w, key_w, value_w, out_w, gains, gate_w, up_w, down_w))
        _, outputs = lax.scan(group_step, jnp.zeros((), jnp.float32), (inputs.reshape(groups, -1, model_width), seq_lens, route_groups, gate_values))
        return outputs.reshape(inputs.shape)
    weights = [w.astype(jnp.float32) for w in (query_weight, key_matrix, value_matrix, out_weight, norm_gains, gate_weight, up_weight, down_weight)]
    result, pullback = jax.vjp(forward, tokens.astype(jnp.float32), *weights)
    gradients = pullback(cotangent.astype(jnp.float32))
    return (result.astype(jnp.bfloat16), gradients[0].astype(jnp.bfloat16), gradients[1], gradients[2], gradients[3], gradients[4], gradients[5], gradients[6], gradients[7], gradients[8])
```

```python
import functools

import jax
import jax.numpy as jnp
from jax import lax
from jax.experimental import pallas as pl
from jax.experimental.pallas import tpu as pltpu
from jax.sharding import PartitionSpec as P

HEAD_DIM = 64
EXPERTS = 16
MAXLEN = 512
EPSILON = 1e-06
BRANCH_SCALE = 0.22
ROPE_BASE = 10000.0
ROWS = 256
LANES = 128
CHUNKS = 2
MIB = 1 << 20
BF16 = jnp.bfloat16
F32 = jnp.float32


def dot_nn(left, right):
    return lax.dot_general(left, right, (((1,), (0,)), ((), ())), preferred_element_type=F32)


def dot_nt(left, right):
    return lax.dot_general(left, right, (((1,), (1,)), ((), ())), preferred_element_type=F32)


def dot_tn(left, right):
    return lax.dot_general(left, right, (((0,), (0,)), ((), ())), preferred_element_type=F32)


def seq_layout(lengths, row_total):
    places = jnp.arange(row_total, dtype=jnp.int32)
    ends = jnp.cumsum(lengths)
    starts = ends - lengths
    segment = jnp.sum((places[:, None] >= ends[None, :]).astype(jnp.int32), axis=1)
    chosen = segment[:, None] == jnp.arange(lengths.shape[0], dtype=jnp.int32)[None, :]
    opening = jnp.sum(jnp.where(chosen, starts[None, :], 0), axis=1)
    return (opening, places - opening)


def rotary_tables(position, head_size):
    halfway = head_size // 2
    ladder = jnp.arange(halfway, dtype=F32)
    inverse = jnp.exp(ladder * (-2.0 * jnp.log(ROPE_BASE) / head_size))
    angles = position.astype(F32)[:, None] * inverse[None, :]
    cos_half, sine_half = (jnp.cos(angles), jnp.sin(angles))
    copies = LANES // head_size
    return (
        jnp.concatenate([cos_half, cos_half] * copies, axis=1),
        jnp.concatenate([-sine_half, sine_half] * copies, axis=1),
    )


def rotate_lanes(values, cos_rows, sine_rows):
    lane = lax.broadcasted_iota(jnp.int32, cos_rows.shape, 1)
    first = lane % HEAD_DIM < HEAD_DIM // 2
    parts = []
    for at in range(0, values.shape[1], LANES):
        part = values[:, at : at + LANES]
        partner = jnp.where(
            first,
            pltpu.roll(part, LANES - HEAD_DIM // 2, 1),
            pltpu.roll(part, HEAD_DIM // 2, 1),
        )
        parts.append(part * cos_rows + partner * sine_rows)
    return jnp.concatenate(parts, axis=1)


def key_window(block):
    low = max(0, block * ROWS - ((MAXLEN - 1 + ROWS - 1) // ROWS) * ROWS)
    return (low, (block + 1) * ROWS)


def allowed_pairs(opening_rows, block, low, high):
    shape = (ROWS, high - low)
    query_at = block * ROWS + lax.broadcasted_iota(jnp.int32, shape, 0)
    key_at = low + lax.broadcasted_iota(jnp.int32, shape, 1)
    return (key_at <= query_at) & (key_at >= opening_rows)


def attend_kernel(
    q_width,
    x_ref,
    gain_ref,
    w_ref,
    cos_ref,
    sine_ref,
    opening_ref,
    a_ref,
    q_ref,
    k_ref,
    v_ref,
    o_ref,
    lse_ref,
    lse_cols,
):
    rows_all = x_ref.shape[0]
    kv_width = k_ref.shape[1]
    kv_heads = kv_width // HEAD_DIM
    group = q_width // kv_width
    scale = HEAD_DIM ** (-0.5)
    for block in range(rows_all // ROWS):
        at = pl.ds(block * ROWS, ROWS)
        x = x_ref[at, :].astype(F32)
        r1 = lax.rsqrt(jnp.mean(x * x, axis=1, keepdims=True) + EPSILON)
        a = (x * r1 * gain_ref[...]).astype(BF16)
        a_ref[at, :] = a
        qkv = dot_nn(a, w_ref[...])
        turned = rotate_lanes(
            qkv[:, : q_width + kv_width], cos_ref[at, :], sine_ref[at, :]
        ).astype(BF16)
        q_ref[at, :] = turned[:, :q_width]
        k_ref[at, :] = turned[:, q_width:]
        v_ref[at, :] = qkv[:, q_width + kv_width :].astype(BF16)
    lane = lax.broadcasted_iota(jnp.int32, (ROWS, LANES), 1)
    for block in range(rows_all // ROWS):
        at = pl.ds(block * ROWS, ROWS)
        low, high = key_window(block)
        keep = allowed_pairs(opening_ref[at, :], block, low, high)
        lse = jnp.zeros((ROWS, LANES), F32)
        outs = []
        for j in range(kv_heads):
            head = slice(j * HEAD_DIM, (j + 1) * HEAD_DIM)
            keys = k_ref[low:high, head]
            vals = v_ref[low:high, head]
            for g in range(group):
                h = j * group + g
                s = dot_nt(q_ref[at, h * HEAD_DIM : (h + 1) * HEAD_DIM], keys) * scale
                s = jnp.where(keep, s, -1e30)
                peak = jnp.max(s, axis=1, keepdims=True)
                p = jnp.exp(s - peak)
                total = jnp.sum(p, axis=1, keepdims=True)
                outs.append((dot_nn(p.astype(BF16), vals) / total).astype(BF16))
                lse = jnp.where(lane == h, peak + jnp.log(total), lse)
        o_ref[at, :] = jnp.concatenate(outs, axis=1)
        lse_cols[at, :] = lse
    lse_ref[...] = lse_cols[...].T[: lse_ref.shape[0], :]


def attend_back_kernel(
    q_ref,
    k_ref,
    v_ref,
    go_ref,
    lse_ref,
    cos_ref,
    sine_ref,
    opening_ref,
    x_ref,
    w_ref,
    d_ref,
    da_ref,
    gain_ref,
    dk_acc,
    dv_acc,
    dq_acc,
):
    rows_all, q_width = q_ref.shape
    kv_width = k_ref.shape[1]
    kv_heads = kv_width // HEAD_DIM
    group = q_width // kv_width
    scale = HEAD_DIM ** (-0.5)
    blocks = rows_all // ROWS
    dk_acc[...] = jnp.zeros_like(dk_acc)
    dv_acc[...] = jnp.zeros_like(dv_acc)
    for block in range(blocks):
        at = pl.ds(block * ROWS, ROWS)
        low, high = key_window(block)
        shape = (high - low, ROWS)
        query_at = block * ROWS + lax.broadcasted_iota(jnp.int32, shape, 1)
        key_at = low + lax.broadcasted_iota(jnp.int32, shape, 0)
        keep = (key_at <= query_at) & (key_at >= opening_ref[:, at])
        for j in range(kv_heads):
            head = slice(j * HEAD_DIM, (j + 1) * HEAD_DIM)
            keys = k_ref[low:high, head]
            vals = v_ref[low:high, head]
            dk = jnp.zeros((high - low, HEAD_DIM), F32)
            dv = jnp.zeros((high - low, HEAD_DIM), F32)
            for g in range(group):
                h = j * group + g
                mine = slice(h * HEAD_DIM, (h + 1) * HEAD_DIM)
                q = q_ref[at, mine]
                go = go_ref[at, mine]
                s = dot_nt(keys, q) * scale
                p = jnp.where(keep, jnp.exp(jnp.minimum(s - lse_ref[h : h + 1, at], 1.0)), 0.0)
                dp = dot_nt(vals, go)
                inner = jnp.sum(p * dp, axis=0, keepdims=True)
                ds = (p * (dp - inner)).astype(BF16)
                dq_acc[at, mine] = dot_tn(ds, keys) * scale
                dk = dk + dot_nn(ds, q)
                dv = dv + dot_nn(p.astype(BF16), go)
            dk_acc[low:high, head] += dk * scale
            dv_acc[low:high, head] += dv
    gain = jnp.zeros((1, x_ref.shape[1]), F32)
    for block in range(blocks):
        at = pl.ds(block * ROWS, ROWS)
        turned = jnp.concatenate([dq_acc[at, :], dk_acc[at, :]], axis=1)
        back = rotate_lanes(turned, cos_ref[at, :], -sine_ref[at, :])
        d = jnp.concatenate([back, dv_acc[at, :]], axis=1).astype(BF16)
        d_ref[at, :] = d
        da = dot_nt(d, w_ref[...])
        da_ref[at, :] = da.astype(BF16)
        x = x_ref[at, :].astype(F32)
        r1 = lax.rsqrt(jnp.mean(x * x, axis=1, keepdims=True) + EPSILON)
        gain = gain + jnp.sum(da * (x * r1), axis=0, keepdims=True)
    gain_ref[...] = gain


def middle_kernel(x_ref, own_ref, other_ref, w_own_ref, w_other_ref, gain_ref, x1_ref, b_ref):
    attn = dot_nt(own_ref[...], w_own_ref[...]) + dot_nt(other_ref[...], w_other_ref[...])
    x1 = x_ref[...].astype(F32) + BRANCH_SCALE * attn
    x1_ref[...] = x1
    r2 = lax.rsqrt(jnp.mean(x1 * x1, axis=1, keepdims=True) + EPSILON)
    b_ref[...] = (x1 * r2 * gain_ref[...]).astype(BF16)


def experts_kernel(
    first, started, b_ref, bt_ref, dy_ref, dyt_ref, gates_ref, w_ref, moe_in, db_in, g_ref, moe_ref, db_ref
):
    step = pl.program_id(0)
    rows_all, width = b_ref.shape

    @pl.when(step == 0)
    def _():
        if started:
            moe_ref[...] = moe_in[...]
            db_ref[...] = db_in[...]
        else:
            moe_ref[...] = jnp.zeros_like(moe_ref)
            db_ref[...] = jnp.zeros_like(db_ref)

    hidden = w_ref.shape[-1]
    gate_w = w_ref[:, 0, 0].reshape(width, hidden)
    up_w = w_ref[:, 0, 1].reshape(width, hidden)
    down_w = w_ref[:, 0, 2].reshape(width, hidden)
    lane = lax.broadcasted_iota(jnp.int32, (ROWS, gates_ref.shape[1]), 1)
    weighted, gate_grads, up_grads = [], [], []
    for block in range(rows_all // ROWS):
        at = pl.ds(block * ROWS, ROWS)
        b = b_ref[at, :]
        route = jnp.sum(
            jnp.where(lane == first + step, gates_ref[at, :], 0.0), axis=1, keepdims=True
        )
        gate = dot_nn(b, gate_w)
        up = dot_nn(b, up_w)
        back = dot_nn(dy_ref[at, :], down_w) * (route * BRANCH_SCALE)
        sig = jax.nn.sigmoid(gate)
        silu = gate * sig
        h = (silu * up * route).astype(BF16)
        dg = (back * up * sig * (1.0 + gate * (1.0 - sig))).astype(BF16)
        du = (back * silu).astype(BF16)
        moe_ref[at, :] += dot_nt(h, down_w)
        db_ref[at, :] += dot_nt(dg, gate_w) + dot_nt(du, up_w)
        weighted.append(h)
        gate_grads.append(dg)
        up_grads.append(du)
    shards, _, _, per_shard, _ = g_ref.shape
    shape = (shards, per_shard, hidden)
    g_ref[:, 0, 0] = dot_nn(bt_ref[...], jnp.concatenate(gate_grads, axis=0)).astype(BF16).reshape(shape)
    g_ref[:, 0, 1] = dot_nn(bt_ref[...], jnp.concatenate(up_grads, axis=0)).astype(BF16).reshape(shape)
    down_grad = dot_nn(dyt_ref[...], jnp.concatenate(weighted, axis=0)) * BRANCH_SCALE
    g_ref[:, 0, 2] = down_grad.astype(BF16).reshape(shape)


def whole(shape):
    return pl.BlockSpec(shape, lambda *_: (0,) * len(shape), pipeline_mode=pl.Buffered(1))


def run_experts(first, b, bt, dy, dyt, gates, weights, carried):
    rows_all, width = b.shape
    shards, count, kinds, per_shard, hidden = weights.shape
    block = (shards, 1, kinds, per_shard, hidden)
    started = carried is not None
    full = jax.ShapeDtypeStruct((rows_all, width), F32)
    moved = lambda e: (0, e, 0, 0, 0)
    if not started:
        carried = (jnp.zeros((8, LANES), F32),) * 2
    flops = 9 * 2 * rows_all * width * hidden * count
    return pl.pallas_call(
        functools.partial(experts_kernel, first, started),
        grid=(count,),
        in_specs=[whole(t.shape) for t in (b, bt, dy, dyt, gates)]
        + [pl.BlockSpec(block, moved)]
        + [whole(t.shape) for t in carried],
        out_specs=[
            pl.BlockSpec(block, moved),
            whole((rows_all, width)),
            whole((rows_all, width)),
        ],
        out_shape=[jax.ShapeDtypeStruct(weights.shape, BF16), full, full],
        compiler_params=pltpu.CompilerParams(vmem_limit_bytes=56 * MIB),
        cost_estimate=pl.CostEstimate(
            flops=flops, bytes_accessed=4 * weights.size + 24 * MIB, transcendentals=0
        ),
        name="experts",
    )(b, bt, dy, dyt, gates, weights, *carried)


def per_device(
    tokens,
    seq_lens,
    routes,
    route_gates,
    query_weight,
    key_matrix,
    value_matrix,
    out_weight,
    norm_gains,
    gate_weight,
    up_weight,
    down_weight,
    cotangent,
):
    local_rows, width = tokens.shape
    rows_all = local_rows * 2
    shards = lax.axis_size("fsdp")
    per_shard = width // shards
    q_width = query_weight.shape[1]
    kv_width = key_matrix.shape[1]
    qkv_width = q_width + 2 * kv_width
    place = lax.axis_index("tp")
    mine_at = place * local_rows
    other_at = (1 - place) * local_rows

    def swap(values):
        return lax.ppermute(values, "tp", [(0, 1), (1, 0)])

    def both(own, other):
        return jnp.where(
            place == 0,
            jnp.concatenate([own, other], axis=0),
            jnp.concatenate([other, own], axis=0),
        )

    attn_local = jnp.concatenate(
        [
            query_weight,
            key_matrix,
            value_matrix,
            out_weight,
            swap(out_weight),
            jnp.pad(norm_gains.T, ((0, 0), (0, LANES - 2))),
        ],
        axis=1,
    )
    attn_w = lax.all_gather(attn_local, "fsdp", axis=0, tiled=True)
    gain_rows = attn_w[:, qkv_width + 2 * q_width :][:, :2].T.astype(F32)
    expert_local = jnp.stack([gate_weight, up_weight, down_weight], axis=1)
    per_chunk = EXPERTS // CHUNKS
    small_shards = per_shard % 16 != 0
    expert_w = []
    for chunk in range(CHUNKS):
        part = lax.all_gather(
            expert_local[chunk * per_chunk : (chunk + 1) * per_chunk], "fsdp", axis=0, tiled=False
        )
        if small_shards:
            part = part.transpose(1, 2, 0, 3, 4).reshape((1,) + part.shape[1:3] + (width, -1))
        expert_w.append(part)

    x_full = both(tokens, swap(tokens))
    dy_full = both(cotangent, swap(cotangent))
    dy_t = dy_full.T
    opening, position = seq_layout(seq_lens[0], rows_all)
    cos_table, sine_table = rotary_tables(position, HEAD_DIM)
    gates = jnp.sum(
        jnp.where(
            routes[:, :, None] == jnp.arange(LANES, dtype=jnp.int32)[None, None, :],
            route_gates[:, :, None],
            0.0,
        ),
        axis=1,
    )

    heads = q_width // HEAD_DIM
    rows_of = lambda n, t: jax.ShapeDtypeStruct((rows_all, n), t)
    normed_one, q_rows, k_rows, v_rows, o_own, lse = pl.pallas_call(
        functools.partial(attend_kernel, q_width),
        grid=(1,),
        in_specs=[
            whole((rows_all, width)),
            whole((1, width)),
            whole((width, qkv_width)),
            whole((rows_all, LANES)),
            whole((rows_all, LANES)),
            whole((rows_all, 1)),
        ],
        out_specs=[
            whole((rows_all, width)),
            whole((rows_all, q_width)),
            whole((rows_all, kv_width)),
            whole((rows_all, kv_width)),
            whole((rows_all, q_width)),
            whole((heads, rows_all)),
        ],
        out_shape=[
            rows_of(width, BF16),
            rows_of(q_width, BF16),
            rows_of(kv_width, BF16),
            rows_of(kv_width, BF16),
            rows_of(q_width, BF16),
            jax.ShapeDtypeStruct((heads, rows_all), F32),
        ],
        scratch_shapes=[pltpu.VMEM((rows_all, LANES), F32)],
        compiler_params=pltpu.CompilerParams(vmem_limit_bytes=48 * MIB),
        cost_estimate=pl.CostEstimate(
            flops=8 * rows_all * width * qkv_width, bytes_accessed=12 * MIB, transcendentals=0
        ),
        name="attend",
    )(x_full, gain_rows[:1], attn_w, cos_table, sine_table, opening[:, None])

    o_other = swap(o_own)
    steps = rows_all // ROWS
    by_rows = lambda n: pl.BlockSpec((ROWS, n), lambda i: (i, 0))
    first_out = qkv_width // q_width
    middle, normed_two = pl.pallas_call(
        middle_kernel,
        grid=(steps,),
        in_specs=[
            by_rows(width),
            by_rows(q_width),
            by_rows(q_width),
            pl.BlockSpec((width, q_width), lambda i: (0, first_out)),
            pl.BlockSpec((width, q_width), lambda i: (0, first_out + 1)),
            pl.BlockSpec((1, width), lambda i: (0, 0)),
        ],
        out_specs=[by_rows(width), by_rows(width)],
        out_shape=[rows_of(width, F32), rows_of(width, BF16)],
        compiler_params=pltpu.CompilerParams(vmem_limit_bytes=32 * MIB),
        cost_estimate=pl.CostEstimate(
            flops=4 * rows_all * width * q_width, bytes_accessed=14 * MIB, transcendentals=0
        ),
        name="middle",
    )(x_full, o_own, o_other, attn_w, attn_w, gain_rows[1:])

    normed_two_t = normed_two.T
    carried = None
    expert_parts = []
    for chunk in range(CHUNKS):
        grads, moe, grad_two = run_experts(
            chunk * per_chunk,
            normed_two,
            normed_two_t,
            dy_full,
            dy_t,
            gates,
            expert_w[chunk],
            carried,
        )
        carried = (moe, grad_two)
        if small_shards:
            grads = grads.reshape(per_chunk, 3, shards, per_shard, -1).transpose(2, 0, 1, 3, 4)
        expert_parts.append(
            lax.psum_scatter(grads, "fsdp", scatter_dimension=0, tiled=False)
        )
    expert_grads = jnp.concatenate(expert_parts, axis=0).astype(F32)

    def own_rows(values):
        return lax.dynamic_slice_in_dim(values, mine_at, local_rows, axis=0)

    def other_rows(values):
        return lax.dynamic_slice_in_dim(values, other_at, local_rows, axis=0)

    grad_two_own = own_rows(grad_two) + swap(other_rows(grad_two).astype(BF16)).astype(F32)
    middle_own = own_rows(middle)
    scale_two = lax.rsqrt(jnp.mean(middle_own * middle_own, axis=1, keepdims=True) + EPSILON)
    unit_two = middle_own * scale_two
    scaled_two = grad_two_own * gain_rows[1]
    grad_middle = cotangent.astype(F32) + scale_two * (
        scaled_two - unit_two * jnp.mean(scaled_two * unit_two, axis=1, keepdims=True)
    )
    gain_two = jnp.sum(grad_two_own * unit_two, axis=0, keepdims=True)
    grad_attn = (BRANCH_SCALE * grad_middle).astype(BF16)
    out_own = attn_w[:, qkv_width : qkv_width + q_width]
    out_other = attn_w[:, qkv_width + q_width : qkv_width + 2 * q_width]
    go_send = jnp.dot(grad_attn, out_other, preferred_element_type=F32).astype(BF16)
    go_other = swap(go_send)
    go_own = jnp.dot(grad_attn, out_own, preferred_element_type=F32).astype(BF16)
    go_full = both(go_own, go_other)
    grad_attn_full = both(grad_attn, swap(grad_attn))
    moe_own = own_rows(moe) + swap(other_rows(moe).astype(BF16)).astype(F32)
    layer_out = (middle_own + BRANCH_SCALE * moe_own).astype(BF16)

    d_qkv, grad_one, gain_one = pl.pallas_call(
        attend_back_kernel,
        grid=(1,),
        in_specs=[
            whole((rows_all, q_width)),
            whole((rows_all, kv_width)),
            whole((rows_all, kv_width)),
            whole((rows_all, q_width)),
            whole((heads, rows_all)),
            whole((rows_all, LANES)),
            whole((rows_all, LANES)),
            whole((1, rows_all)),
            whole((rows_all, width)),
            whole((width, qkv_width)),
        ],
        out_specs=[whole((rows_all, qkv_width)), whole((rows_all, width)), whole((1, width))],
        out_shape=[
            rows_of(qkv_width, BF16),
            rows_of(width, BF16),
            jax.ShapeDtypeStruct((1, width), F32),
        ],
        scratch_shapes=[
            pltpu.VMEM((rows_all, kv_width), F32),
            pltpu.VMEM((rows_all, kv_width), F32),
            pltpu.VMEM((rows_all, q_width), F32),
        ],
        compiler_params=pltpu.CompilerParams(vmem_limit_bytes=48 * MIB),
        cost_estimate=pl.CostEstimate(
            flops=16 * rows_all * width * qkv_width, bytes_accessed=12 * MIB, transcendentals=0
        ),
        name="attend_back",
    )(
        q_rows,
        k_rows,
        v_rows,
        go_full,
        lse,
        cos_table,
        sine_table,
        opening[None, :],
        x_full,
        attn_w,
    )

    grad_one_own = own_rows(grad_one).astype(F32) + swap(other_rows(grad_one)).astype(F32)
    gain_part = jnp.concatenate([gain_one, gain_two], axis=0)
    gain_sum = gain_part + swap(gain_part)
    grad_qkv_w = dot_tn(normed_one, d_qkv)
    grad_out_w = dot_tn(grad_attn_full, o_own)
    attn_parts = jnp.concatenate(
        [grad_qkv_w, grad_out_w, jnp.pad(gain_sum.T, ((0, 0), (0, LANES - 2)))], axis=1
    ).astype(BF16)
    attn_grads = lax.psum_scatter(attn_parts, "fsdp", scatter_dimension=0, tiled=True).astype(F32)

    inputs = tokens.astype(F32)
    scale_one = lax.rsqrt(jnp.mean(inputs * inputs, axis=1, keepdims=True) + EPSILON)
    unit_one = inputs * scale_one
    scaled_one = grad_one_own * gain_rows[0]
    grad_tokens = (
        grad_middle
        + scale_one
        * (scaled_one - unit_one * jnp.mean(scaled_one * unit_one, axis=1, keepdims=True))
    ).astype(BF16)
    return (
        layer_out,
        grad_tokens,
        attn_grads[:, :q_width],
        attn_grads[:, q_width : q_width + kv_width],
        attn_grads[:, q_width + kv_width : qkv_width],
        attn_grads[:, qkv_width : qkv_width + q_width],
        attn_grads[:, qkv_width + q_width :][:, :2].T,
        expert_grads[:, 0],
        expert_grads[:, 1],
        expert_grads[:, 2],
    )


def solution(mesh):
    in_specs = (
        P(("fsdp", "tp"), None),
        P("fsdp", None),
        P("fsdp", None),
        P("fsdp", None),
        P("fsdp", "tp"),
        P("fsdp", "tp"),
        P("fsdp", "tp"),
        P("fsdp", "tp"),
        P(None, "fsdp"),
        P(None, "fsdp", "tp"),
        P(None, "fsdp", "tp"),
        P(None, "fsdp", "tp"),
        P(("fsdp", "tp"), None),
    )
    out_specs = (
        P(("fsdp", "tp"), None),
        P(("fsdp", "tp"), None),
        P("fsdp", "tp"),
        P("fsdp", "tp"),
        P("fsdp", "tp"),
        P("fsdp", "tp"),
        P(None, "fsdp"),
        P(None, "fsdp", "tp"),
        P(None, "fsdp", "tp"),
        P(None, "fsdp", "tp"),
    )
    return jax.shard_map(
        per_device, mesh=mesh, in_specs=in_specs, out_specs=out_specs, check_vma=False
    )
```

```python
import functools

import jax
import jax.numpy as jnp
from jax import lax
from jax.experimental import pallas as pl
from jax.experimental.pallas import tpu as pltpu
from jax.sharding import PartitionSpec as P

HEAD_DIM = 64
EXPERTS = 16
MAXLEN = 512
EPSILON = 1e-06
BRANCH_SCALE = 0.22
ROPE_BASE = 10000.0
ROWS = 256
LANES = 128
GATHERED = (12, 4)
SPLIT = (4, 4, 4, 4)
PERMUTED = (True, True, True, True)
DIRECT_MAX = 16
MIB = 1 << 20
BF16 = jnp.bfloat16
F32 = jnp.float32


def dot_nn(left, right):
    return lax.dot_general(left, right, (((1,), (0,)), ((), ())), preferred_element_type=F32)


def dot_nt(left, right):
    return lax.dot_general(left, right, (((1,), (1,)), ((), ())), preferred_element_type=F32)


def dot_tn(left, right):
    return lax.dot_general(left, right, (((0,), (0,)), ((), ())), preferred_element_type=F32)


def seq_layout(lengths, row_total):
    places = jnp.arange(row_total, dtype=jnp.int32)
    ends = jnp.cumsum(lengths)
    starts = ends - lengths
    segment = jnp.sum((places[:, None] >= ends[None, :]).astype(jnp.int32), axis=1)
    chosen = segment[:, None] == jnp.arange(lengths.shape[0], dtype=jnp.int32)[None, :]
    opening = jnp.sum(jnp.where(chosen, starts[None, :], 0), axis=1)
    return (opening, places - opening)


def rotary_tables(position, head_size):
    halfway = head_size // 2
    ladder = jnp.arange(halfway, dtype=F32)
    inverse = jnp.exp(ladder * (-2.0 * jnp.log(ROPE_BASE) / head_size))
    angles = position.astype(F32)[:, None] * inverse[None, :]
    cos_half, sine_half = (jnp.cos(angles), jnp.sin(angles))
    copies = LANES // head_size
    return (
        jnp.concatenate([cos_half, cos_half] * copies, axis=1),
        jnp.concatenate([-sine_half, sine_half] * copies, axis=1),
    )


def rotate_lanes(values, cos_rows, sine_rows):
    lane = lax.broadcasted_iota(jnp.int32, cos_rows.shape, 1)
    first = lane % HEAD_DIM < HEAD_DIM // 2
    parts = []
    for at in range(0, values.shape[1], LANES):
        part = values[:, at : at + LANES]
        partner = jnp.where(
            first,
            pltpu.roll(part, LANES - HEAD_DIM // 2, 1),
            pltpu.roll(part, HEAD_DIM // 2, 1),
        )
        parts.append(part * cos_rows + partner * sine_rows)
    return jnp.concatenate(parts, axis=1)


def key_window(block):
    low = max(0, block * ROWS - ((MAXLEN - 1 + ROWS - 1) // ROWS) * ROWS)
    return (low, (block + 1) * ROWS)


def allowed_pairs(opening_rows, block, low, high):
    shape = (ROWS, high - low)
    query_at = block * ROWS + lax.broadcasted_iota(jnp.int32, shape, 0)
    key_at = low + lax.broadcasted_iota(jnp.int32, shape, 1)
    return (key_at <= query_at) & (key_at >= opening_rows)


def attend_kernel(
    q_width,
    x_ref,
    gain_ref,
    w_ref,
    cos_ref,
    sine_ref,
    opening_ref,
    at_ref,
    q_ref,
    k_ref,
    v_ref,
    o_ref,
    lse_ref,
    gain_rows_ref,
    lse_cols,
):
    rows_all = x_ref.shape[0]
    gain_rows_ref[...] = gain_ref[...].astype(F32).T[: gain_rows_ref.shape[0], :]
    kv_width = k_ref.shape[1]
    kv_heads = kv_width // HEAD_DIM
    group = q_width // kv_width
    scale = HEAD_DIM ** (-0.5)
    for block in range(rows_all // ROWS):
        at = pl.ds(block * ROWS, ROWS)
        x = x_ref[at, :].astype(F32)
        r1 = lax.rsqrt(jnp.mean(x * x, axis=1, keepdims=True) + EPSILON)
        a = (x * r1 * gain_rows_ref[0:1, :]).astype(BF16)
        at_ref[:, at] = a.T
        qkv = dot_nn(a, w_ref[...])
        turned = rotate_lanes(
            qkv[:, : q_width + kv_width], cos_ref[at, :], sine_ref[at, :]
        ).astype(BF16)
        q_ref[at, :] = turned[:, :q_width]
        k_ref[at, :] = turned[:, q_width:]
        v_ref[at, :] = qkv[:, q_width + kv_width :].astype(BF16)
    lane = lax.broadcasted_iota(jnp.int32, (ROWS, LANES), 1)
    for block in range(rows_all // ROWS):
        at = pl.ds(block * ROWS, ROWS)
        low, high = key_window(block)
        keep = allowed_pairs(opening_ref[at, :], block, low, high)
        lse = jnp.zeros((ROWS, LANES), F32)
        outs = []
        for j in range(kv_heads):
            head = slice(j * HEAD_DIM, (j + 1) * HEAD_DIM)
            keys = k_ref[low:high, head]
            vals = v_ref[low:high, head]
            for g in range(group):
                h = j * group + g
                s = dot_nt(q_ref[at, h * HEAD_DIM : (h + 1) * HEAD_DIM], keys) * scale
                s = jnp.where(keep, s, -1e30)
                peak = jnp.max(s, axis=1, keepdims=True)
                p = jnp.exp(s - peak)
                total = jnp.sum(p, axis=1, keepdims=True)
                outs.append((dot_nn(p.astype(BF16), vals) / total).astype(BF16))
                lse = jnp.where(lane == h, peak + jnp.log(total), lse)
        o_ref[at, :] = jnp.concatenate(outs, axis=1)
        lse_cols[at, :] = lse
    lse_ref[...] = lse_cols[...].T[: lse_ref.shape[0], :]


def attend_back_kernel(
    here_ref,
    q_ref,
    k_ref,
    v_ref,
    go_own_ref,
    go_other_ref,
    lse_ref,
    cos_ref,
    sine_ref,
    opening_ref,
    x_ref,
    w_ref,
    d_ref,
    da_own_ref,
    da_send_ref,
    gain_ref,
    dk_acc,
    dv_acc,
    dq_acc,
    go_ref,
):
    here = here_ref[0]
    local_rows = go_own_ref.shape[0]
    go_ref[pl.ds(pl.multiple_of(here * local_rows, local_rows), local_rows), :] = go_own_ref[...]
    go_ref[pl.ds(pl.multiple_of((1 - here) * local_rows, local_rows), local_rows), :] = (
        go_other_ref[...]
    )
    rows_all, q_width = q_ref.shape
    kv_width = k_ref.shape[1]
    kv_heads = kv_width // HEAD_DIM
    group = q_width // kv_width
    scale = HEAD_DIM ** (-0.5)
    blocks = rows_all // ROWS
    dk_acc[...] = jnp.zeros_like(dk_acc)
    dv_acc[...] = jnp.zeros_like(dv_acc)
    for block in range(blocks):
        at = pl.ds(block * ROWS, ROWS)
        low, high = key_window(block)
        shape = (high - low, ROWS)
        query_at = block * ROWS + lax.broadcasted_iota(jnp.int32, shape, 1)
        key_at = low + lax.broadcasted_iota(jnp.int32, shape, 0)
        keep = (key_at <= query_at) & (key_at >= opening_ref[:, at])
        for j in range(kv_heads):
            head = slice(j * HEAD_DIM, (j + 1) * HEAD_DIM)
            keys = k_ref[low:high, head]
            vals = v_ref[low:high, head]
            dk = jnp.zeros((high - low, HEAD_DIM), F32)
            dv = jnp.zeros((high - low, HEAD_DIM), F32)
            for g in range(group):
                h = j * group + g
                mine = slice(h * HEAD_DIM, (h + 1) * HEAD_DIM)
                q = q_ref[at, mine]
                go = go_ref[at, mine]
                s = dot_nt(keys, q) * scale
                p = jnp.where(keep, jnp.exp(s - lse_ref[h : h + 1, at]), 0.0)
                dp = dot_nt(vals, go)
                inner = jnp.sum(p * dp, axis=0, keepdims=True)
                ds = (p * (dp - inner)).astype(BF16)
                dq_acc[at, mine] = dot_tn(ds, keys) * scale
                dk = dk + dot_nn(ds, q)
                dv = dv + dot_nn(p.astype(BF16), go)
            dk_acc[low:high, head] += dk * scale
            dv_acc[low:high, head] += dv
    gain = jnp.zeros((1, x_ref.shape[1]), F32)
    for block in range(blocks):
        at = pl.ds(block * ROWS, ROWS)
        turned = jnp.concatenate([dq_acc[at, :], dk_acc[at, :]], axis=1)
        back = rotate_lanes(turned, cos_ref[at, :], -sine_ref[at, :])
        d = jnp.concatenate([back, dv_acc[at, :]], axis=1).astype(BF16)
        d_ref[at, :] = d
        da = dot_nt(d, w_ref[...])
        half, inside = divmod(block * ROWS, local_rows)
        da_rows = da.astype(BF16)

        @pl.when(here == half)
        def _():
            da_own_ref[inside : inside + ROWS, :] = da_rows

        @pl.when(here != half)
        def _():
            da_send_ref[inside : inside + ROWS, :] = da_rows

        x = x_ref[at, :].astype(F32)
        r1 = lax.rsqrt(jnp.mean(x * x, axis=1, keepdims=True) + EPSILON)
        gain = gain + jnp.sum(da * (x * r1), axis=0, keepdims=True)
    gain_ref[...] = gain


def attn_grads_kernel(here_ref, at_ref, d_ref, own_ref, other_ref, o_ref, gain_ref, parts_ref):
    local_rows = own_ref.shape[0]
    mine = pl.ds(pl.multiple_of(here_ref[0] * local_rows, local_rows), local_rows)
    others = pl.ds(pl.multiple_of((1 - here_ref[0]) * local_rows, local_rows), local_rows)
    qkv_width, q_width = d_ref.shape[1], o_ref.shape[1]
    parts_ref[:, :qkv_width] = dot_nn(at_ref[...], d_ref[...]).astype(BF16)
    out_grad = dot_tn(own_ref[...], o_ref[mine, :]) + dot_tn(other_ref[...], o_ref[others, :])
    parts_ref[:, qkv_width : qkv_width + q_width] = out_grad.astype(BF16)
    parts_ref[:, qkv_width + q_width :] = gain_ref[...].astype(BF16)


def middle_back_kernel(
    here_ref,
    db_ref,
    got_ref,
    x1_ref,
    dy_ref,
    gain_ref,
    w_own_ref,
    w_other_ref,
    dx1_ref,
    attn_ref,
    send_ref,
    own_ref,
    gain_grad_ref,
):
    db = db_ref[...] + got_ref[...].astype(F32)
    x1 = x1_ref[...]
    r2 = lax.rsqrt(jnp.mean(x1 * x1, axis=1, keepdims=True) + EPSILON)
    u2 = x1 * r2
    e2 = db * gain_ref[1:2, :]
    dx1 = dy_ref[...].astype(F32) + r2 * (e2 - u2 * jnp.mean(e2 * u2, axis=1, keepdims=True))
    dx1_ref[...] = dx1
    attn = (BRANCH_SCALE * dx1).astype(BF16)
    attn_ref[...] = attn
    send_ref[...] = dot_nn(attn, w_other_ref[...]).astype(BF16)
    own_ref[...] = dot_nn(attn, w_own_ref[...]).astype(BF16)
    gain_grad = jnp.sum(db * u2, axis=0, keepdims=True)

    @pl.when(pl.program_id(0) == 0)
    def _():
        gain_grad_ref[...] = gain_grad

    @pl.when(pl.program_id(0) > 0)
    def _():
        gain_grad_ref[...] += gain_grad


def middle_kernel(x_ref, own_ref, other_ref, w_own_ref, w_other_ref, gain_ref, x1_ref, b_ref, bt_ref):
    attn = dot_nt(own_ref[...], w_own_ref[...]) + dot_nt(other_ref[...], w_other_ref[...])
    x1 = x_ref[...].astype(F32) + BRANCH_SCALE * attn
    x1_ref[...] = x1
    r2 = lax.rsqrt(jnp.mean(x1 * x1, axis=1, keepdims=True) + EPSILON)
    b = (x1 * r2 * gain_ref[1:2, :]).astype(BF16)
    b_ref[...] = b
    bt_ref[...] = b.T


def piece_of(d):
    if d == 0:
        return 0, 0
    n = (d & -d).bit_length()
    return n, d >> n


def experts_kernel(
    started,
    last,
    stages,
    place_ref,
    b_ref,
    bt_ref,
    dy_ref,
    dyt_ref,
    gates_ref,
    w_ref,
    db_in,
    *refs,
):
    g_refs, refs = refs[: stages + 1], refs[stages + 1 :]
    h_ref, db_ref, refs = refs[0], refs[1], refs[2:]
    g_scr = refs[-1]
    step = pl.program_id(0)
    rows_all, width = b_ref.shape

    @pl.when(step == 0)
    def _():
        db_ref[...] = db_in[...] if started else jnp.zeros_like(db_ref)

    hidden = w_ref.shape[-1]
    gate_w, up_w, down_w = [w_ref[:, kind, 0].reshape(width, hidden) for kind in range(3)]
    lane = lax.broadcasted_iota(jnp.int32, (ROWS, gates_ref.shape[1]), 1)
    weighted, gate_grads, up_grads = [], [], []
    for block in range(rows_all // ROWS):
        at = pl.ds(block * ROWS, ROWS)
        b = b_ref[at, :]
        route = jnp.sum(
            jnp.where(lane == place_ref[1] + step, gates_ref[at, :], 0.0), axis=1, keepdims=True
        )
        gate = dot_nn(b, gate_w)
        up = dot_nn(b, up_w)
        back = dot_nn(dy_ref[at, :], down_w) * (route * BRANCH_SCALE)
        sig = jax.nn.sigmoid(gate)
        silu = gate * sig
        h = (silu * up * route).astype(BF16)
        dg = (back * up * sig * (1.0 + gate * (1.0 - sig))).astype(BF16)
        du = (back * silu).astype(BF16)
        h_ref[at, :] = h
        db_ref[at, :] += dot_nt(dg, gate_w) + dot_nt(du, up_w)
        weighted.append(h)
        gate_grads.append(dg)
        up_grads.append(du)
    for kind, left_ref, right, scale in (
        (0, bt_ref, gate_grads, None),
        (1, bt_ref, up_grads, None),
        (2, dyt_ref, weighted, BRANCH_SCALE),
    ):
        grad = dot_nn(left_ref[...], jnp.concatenate(right, axis=0))
        if scale is not None:
            grad = grad * scale
        g_scr[kind] = grad.astype(BF16).reshape(g_scr.shape[1:])
    for d in range(g_scr.shape[1]):
        n, at = piece_of(d) if stages else (0, d)
        source = d ^ place_ref[0] if stages else d
        for kind in range(3):
            g_refs[n][at, kind, 0] = g_scr[kind, source]

    if last:

        @pl.when(step == pl.num_programs(0) - 1)
        def _():
            send_ref = refs[0]
            rows = send_ref.shape[0]
            start = pl.multiple_of(place_ref[2], rows)
            send_ref[...] = db_ref[pl.ds(start, rows), :].astype(BF16)


def output_kernel(counts, *refs):
    chunks = len(counts)
    h_refs, w_refs, (moe_ref, acc) = refs[:chunks], refs[chunks : 2 * chunks], refs[2 * chunks :]
    step = pl.program_id(0)
    width, hidden = acc.shape[1], w_refs[0].shape[-1]

    @pl.when(step == 0)
    def _():
        acc[...] = jnp.zeros_like(acc)

    def add(held):
        acc[...] += sum(
            dot_nt(h_refs[n][...], w_refs[n][:, 0, 0].reshape(width, hidden)) for n in held
        )

    limits = sorted(set(counts))
    for low, high in zip([0] + limits, limits):
        held = [n for n in range(chunks) if counts[n] >= high]
        pl.when((step >= low) & (step < high))(functools.partial(add, held))

    @pl.when(step == pl.num_programs(0) - 1)
    def _():
        moe_ref[...] = acc[...].astype(BF16)


def whole(shape):
    return pl.BlockSpec(shape, lambda *_: (0,) * len(shape), pipeline_mode=pl.Buffered(1))


def run_experts(
    place, b, bt, dy, dyt, gates, weights, first, count, parts, stages, carried, last
):
    rows_all, width = b.shape
    shards, kinds, _, per_shard, hidden = weights.shape
    out_rows = width // parts
    sizes = [1] + [1 << (stages - n) for n in range(1, stages + 1)] if stages else [parts]
    local_rows = rows_all // 2
    started = carried is not None
    if not started:
        carried = jnp.zeros((8, LANES), F32)
    results = pl.pallas_call(
        functools.partial(experts_kernel, started, last, stages),
        grid_spec=pltpu.PrefetchScalarGridSpec(
            num_scalar_prefetch=1,
            grid=(count,),
            in_specs=[whole(t.shape) for t in (b, bt, dy, dyt, gates)]
            + [
                pl.BlockSpec(
                    (shards, kinds, 1, per_shard, hidden),
                    lambda e, place: (0, 0, first + e, 0, 0),
                ),
                whole(carried.shape),
            ],
            out_specs=[
                pl.BlockSpec(
                    (size, kinds, 1, out_rows, hidden), lambda e, place: (0, 0, e, 0, 0)
                )
                for size in sizes
            ]
            + [
                pl.BlockSpec((rows_all, hidden), lambda e, place: (0, e)),
                whole((rows_all, width)),
            ]
            + [whole((local_rows, width))] * last,
            scratch_shapes=[pltpu.VMEM((kinds, parts, out_rows, hidden), BF16)],
        ),
        out_shape=[
            jax.ShapeDtypeStruct((size, kinds, count, out_rows, hidden), BF16) for size in sizes
        ]
        + [
            jax.ShapeDtypeStruct((rows_all, count * hidden), BF16),
            jax.ShapeDtypeStruct((rows_all, width), F32),
        ]
        + [jax.ShapeDtypeStruct((local_rows, width), BF16)] * last,
        compiler_params=pltpu.CompilerParams(vmem_limit_bytes=48 * MIB),
        cost_estimate=pl.CostEstimate(
            flops=8 * 2 * rows_all * width * hidden * count,
            bytes_accessed=4 * kinds * count * width * hidden + 18 * MIB,
            transcendentals=0,
        ),
        name="experts",
    )(place, b, bt, dy, dyt, gates, weights, carried)
    pieces = len(sizes)
    return results[:pieces], results[pieces], results[pieces + 1], results[pieces + 2 :]


def run_output(hidden_parts, weight_parts, firsts, rows_all, width):
    shards, _, _, per_shard, hidden = weight_parts[0].shape
    counts = [h.shape[1] // hidden for h in hidden_parts]

    def hidden_spec(count):
        return pl.BlockSpec((rows_all, hidden), lambda e: (0, jnp.minimum(e, count - 1)))

    def weight_spec(first, count):
        return pl.BlockSpec(
            (shards, 1, 1, per_shard, hidden),
            lambda e: (0, 2, first + jnp.minimum(e, count - 1), 0, 0),
        )

    return pl.pallas_call(
        functools.partial(output_kernel, counts),
        grid=(max(counts),),
        in_specs=[hidden_spec(count) for count in counts]
        + [weight_spec(first, count) for first, count in zip(firsts, counts)],
        out_specs=whole((rows_all, width)),
        out_shape=jax.ShapeDtypeStruct((rows_all, width), BF16),
        scratch_shapes=[pltpu.VMEM((rows_all, width), F32)],
        compiler_params=pltpu.CompilerParams(vmem_limit_bytes=40 * MIB),
        cost_estimate=pl.CostEstimate(
            flops=2 * rows_all * width * hidden * sum(counts),
            bytes_accessed=18 * MIB,
            transcendentals=0,
        ),
        name="expert_output",
    )(*hidden_parts, *weight_parts)


class PieceSum:
    def __init__(self, pieces, shards):
        self.shards = shards
        self.stages = len(pieces) - 1
        self.own, self.rest = pieces[0], pieces[1:]
        self.stage = 0
        self.got = self.swap(self.rest[0])

    def swap(self, values):
        bit = 1 << self.stage
        return lax.ppermute(values, "fsdp", [(s, s ^ bit) for s in range(self.shards)])

    def ready(self):
        if self.stage == self.stages - 1:
            return [self.own.astype(F32) + self.got[:1].astype(F32)]
        left = [self.own + self.got[:1]]
        for n, piece in enumerate(self.rest[self.stage + 1 :]):
            left.append(piece + self.got[1 << n :: 2 << n])
        return left

    def send(self, values):
        if self.stage == self.stages - 1:
            self.total = values[0][0]
            self.stage += 1
            return
        self.stage += 1
        self.own = values[0]
        self.rest = [None] * self.stage + values[1:]
        self.got = self.swap(self.rest[self.stage])


def per_device(
    tokens,
    seq_lens,
    routes,
    route_gates,
    query_weight,
    key_matrix,
    value_matrix,
    out_weight,
    norm_gains,
    gate_weight,
    up_weight,
    down_weight,
    cotangent,
):
    local_rows, width = tokens.shape
    rows_all = local_rows * 2
    shards = lax.axis_size("fsdp")
    per_shard = width // shards
    q_width = query_weight.shape[1]
    kv_width = key_matrix.shape[1]
    qkv_width = q_width + 2 * kv_width
    place = lax.axis_index("tp")
    mine_at = place * local_rows
    other_at = (1 - place) * local_rows

    def swap(values):
        return lax.ppermute(values, "tp", [(0, 1), (1, 0)])

    def both(own, other):
        return lax.dynamic_update_slice_in_dim(
            jnp.concatenate([own, own], axis=0), other, other_at, axis=0
        )

    attn_local = jnp.concatenate(
        [
            query_weight,
            key_matrix,
            value_matrix,
            out_weight,
            jnp.pad(norm_gains.T, ((0, 0), (0, LANES - 2))),
        ],
        axis=1,
    )
    attn_w = lax.all_gather(attn_local, "fsdp", axis=0, tiled=True)
    hidden_width = gate_weight.shape[-1]
    expert_w, expert_at = [], []
    start = 0
    for count in GATHERED:
        part = jnp.concatenate(
            [
                w[start : start + count].reshape(-1, hidden_width)
                for w in (gate_weight, up_weight, down_weight)
            ]
        )
        part = lax.all_gather(part, "fsdp", axis=0, tiled=True)
        part = part.reshape(shards, 3, count, per_shard, hidden_width)
        if per_shard % 16 != 0:
            part = part.transpose(1, 2, 0, 3, 4).reshape(1, 3, count, width, hidden_width)
        expert_w.append(part)
        expert_at += [(len(expert_w) - 1, at) for at in range(count)]
        start += count
    stages = shards.bit_length() - 1
    whole_tiles = per_shard % 16 == 0
    direct = 2 <= shards <= DIRECT_MAX and 1 << stages == shards and whole_tiles
    index = lax.axis_index("fsdp") if direct else 0

    x_full = both(tokens, swap(tokens))
    dy_full = both(cotangent, swap(cotangent))
    dy_t = dy_full.T
    opening, position = seq_layout(seq_lens[0], rows_all)
    cos_table, sine_table = rotary_tables(position, HEAD_DIM)
    gates = jnp.sum(
        jnp.where(
            routes[:, :, None] == jnp.arange(LANES, dtype=jnp.int32)[None, None, :],
            route_gates[:, :, None],
            0.0,
        ),
        axis=1,
    )

    out_own, x_full = lax.optimization_barrier(
        (attn_w[:, qkv_width : qkv_width + q_width], x_full)
    )
    out_other = swap(out_own)
    heads = q_width // HEAD_DIM
    rows_of = lambda n, t: jax.ShapeDtypeStruct((rows_all, n), t)
    normed_one_t, q_rows, k_rows, v_rows, o_own, lse, gain_rows = pl.pallas_call(
        functools.partial(attend_kernel, q_width),
        grid=(1,),
        in_specs=[
            whole((rows_all, width)),
            pl.BlockSpec(
                (width, LANES),
                lambda i: (0, (qkv_width + q_width) // LANES),
                pipeline_mode=pl.Buffered(1),
            ),
            whole((width, qkv_width)),
            whole((rows_all, LANES)),
            whole((rows_all, LANES)),
            whole((rows_all, 1)),
        ],
        out_specs=[
            whole((width, rows_all)),
            whole((rows_all, q_width)),
            whole((rows_all, kv_width)),
            whole((rows_all, kv_width)),
            whole((rows_all, q_width)),
            whole((heads, rows_all)),
            whole((8, width)),
        ],
        out_shape=[
            jax.ShapeDtypeStruct((width, rows_all), BF16),
            rows_of(q_width, BF16),
            rows_of(kv_width, BF16),
            rows_of(kv_width, BF16),
            rows_of(q_width, BF16),
            jax.ShapeDtypeStruct((heads, rows_all), F32),
            jax.ShapeDtypeStruct((8, width), F32),
        ],
        scratch_shapes=[pltpu.VMEM((rows_all, LANES), F32)],
        compiler_params=pltpu.CompilerParams(vmem_limit_bytes=48 * MIB),
        cost_estimate=pl.CostEstimate(
            flops=8 * rows_all * width * qkv_width, bytes_accessed=12 * MIB, transcendentals=0
        ),
        name="attend",
    )(x_full, attn_w, attn_w, cos_table, sine_table, opening[:, None])

    o_other = swap(o_own)
    steps = rows_all // ROWS
    by_rows = lambda n: pl.BlockSpec((ROWS, n), lambda i: (i, 0))
    first_out = qkv_width // q_width
    middle, normed_two, normed_two_t = pl.pallas_call(
        middle_kernel,
        grid=(steps,),
        in_specs=[
            by_rows(width),
            by_rows(q_width),
            by_rows(q_width),
            pl.BlockSpec((width, q_width), lambda i: (0, first_out)),
            pl.BlockSpec((width, q_width), lambda i: (0, 0)),
            pl.BlockSpec((8, width), lambda i: (0, 0)),
        ],
        out_specs=[
            by_rows(width),
            by_rows(width),
            pl.BlockSpec((width, ROWS), lambda i: (0, i)),
        ],
        out_shape=[
            rows_of(width, F32),
            rows_of(width, BF16),
            jax.ShapeDtypeStruct((width, rows_all), BF16),
        ],
        compiler_params=pltpu.CompilerParams(vmem_limit_bytes=32 * MIB),
        cost_estimate=pl.CostEstimate(
            flops=4 * rows_all * width * q_width, bytes_accessed=14 * MIB, transcendentals=0
        ),
        name="middle",
    )(x_full, o_own, o_other, attn_w, out_other, gain_rows)

    def advance(anchor, parts):
        parts = [part for part in parts if isinstance(part, PieceSum)]
        if not parts:
            return anchor
        parts = [part for part in parts if part.stage < part.stages]
        if not parts:
            return anchor
        values = [part.ready() for part in parts]
        anchor, values = lax.optimization_barrier((anchor, values))
        for part, value in zip(parts, values):
            part.send(value)
        return anchor

    grad_two = None
    sums, hidden_parts, held_parts, firsts = [], [], [], []
    start = 0
    for count in SPLIT:
        if len(sums) >= 2:
            grad_two = advance(grad_two, sums[:-1])
        permuted = direct and PERMUTED[len(sums)]
        held, first = expert_at[start]
        where = jnp.stack([index, start, other_at]).astype(jnp.int32)
        grads, hidden, grad_two, sent = run_experts(
            where,
            normed_two,
            normed_two_t,
            dy_full,
            dy_t,
            gates,
            expert_w[held],
            first,
            count,
            shards if whole_tiles else 1,
            stages if permuted else 0,
            grad_two,
            start + count == EXPERTS,
        )
        hidden_parts.append(hidden)
        held_parts.append(expert_w[held])
        firsts.append(first)
        if permuted:
            sums.append(PieceSum(grads, shards))
        else:
            grads = grads[0]
            if not whole_tiles:
                grads = grads.reshape(3, count, shards, per_shard, -1).transpose(2, 0, 1, 3, 4)
            grads = lax.psum_scatter(
                grads.reshape(-1, hidden_width), "fsdp", scatter_dimension=0, tiled=True
            )
            sums.append(grads.reshape(3, count, per_shard, hidden_width))
        start += count

    grad_two_other = swap(sent[0])
    grad_two_other = advance(grad_two_other, sums)
    here = place.astype(jnp.int32)[None]
    steps = local_rows // ROWS
    own_block = lambda i, here: (here[0] * steps + i, 0)
    local_block = lambda i, here: (i, 0)
    grad_middle, grad_attn, go_send, go_own, gain_two = pl.pallas_call(
        middle_back_kernel,
        grid_spec=pltpu.PrefetchScalarGridSpec(
            num_scalar_prefetch=1,
            grid=(steps,),
            in_specs=[
                pl.BlockSpec((ROWS, width), own_block),
                pl.BlockSpec((ROWS, width), local_block),
                pl.BlockSpec((ROWS, width), own_block),
                pl.BlockSpec((ROWS, width), local_block),
                whole((8, width)),
                whole((width, q_width)),
                whole((width, q_width)),
            ],
            out_specs=[
                pl.BlockSpec((ROWS, width), local_block),
                pl.BlockSpec((ROWS, width), local_block),
                pl.BlockSpec((ROWS, q_width), local_block),
                pl.BlockSpec((ROWS, q_width), local_block),
                whole((1, width)),
            ],
        ),
        out_shape=[
            jax.ShapeDtypeStruct((local_rows, width), F32),
            jax.ShapeDtypeStruct((local_rows, width), BF16),
            jax.ShapeDtypeStruct((local_rows, q_width), BF16),
            jax.ShapeDtypeStruct((local_rows, q_width), BF16),
            jax.ShapeDtypeStruct((1, width), F32),
        ],
        compiler_params=pltpu.CompilerParams(vmem_limit_bytes=32 * MIB),
        cost_estimate=pl.CostEstimate(
            flops=4 * local_rows * width * q_width, bytes_accessed=12 * MIB, transcendentals=0
        ),
        name="middle_back",
    )(here, grad_two, grad_two_other, middle, cotangent, gain_rows, out_own, out_other)
    go_other = swap(go_send)
    go_other, attn_send = lax.optimization_barrier((go_other, grad_attn))
    grad_attn_other = swap(attn_send)
    go_other = advance(go_other, sums[:2])

    d_qkv, grad_one, grad_one_send, gain_one = pl.pallas_call(
        attend_back_kernel,
        grid=(1,),
        in_specs=[
            pl.BlockSpec(memory_space=pltpu.SMEM),
            whole((rows_all, q_width)),
            whole((rows_all, kv_width)),
            whole((rows_all, kv_width)),
            whole((local_rows, q_width)),
            whole((local_rows, q_width)),
            whole((heads, rows_all)),
            whole((rows_all, LANES)),
            whole((rows_all, LANES)),
            whole((1, rows_all)),
            whole((rows_all, width)),
            whole((width, qkv_width)),
        ],
        out_specs=[
            whole((rows_all, qkv_width)),
            whole((local_rows, width)),
            whole((local_rows, width)),
            whole((1, width)),
        ],
        out_shape=[
            rows_of(qkv_width, BF16),
            jax.ShapeDtypeStruct((local_rows, width), BF16),
            jax.ShapeDtypeStruct((local_rows, width), BF16),
            jax.ShapeDtypeStruct((1, width), F32),
        ],
        scratch_shapes=[
            pltpu.VMEM((rows_all, kv_width), F32),
            pltpu.VMEM((rows_all, kv_width), F32),
            pltpu.VMEM((rows_all, q_width), F32),
            pltpu.VMEM((rows_all, q_width), BF16),
        ],
        compiler_params=pltpu.CompilerParams(vmem_limit_bytes=48 * MIB),
        cost_estimate=pl.CostEstimate(
            flops=16 * rows_all * width * qkv_width, bytes_accessed=12 * MIB, transcendentals=0
        ),
        name="attend_back",
    )(
        here,
        q_rows,
        k_rows,
        v_rows,
        go_own,
        go_other,
        lse,
        cos_table,
        sine_table,
        opening[None, :],
        x_full,
        attn_w,
    )

    grad_one_other = swap(grad_one_send)
    d_qkv = advance(d_qkv, sums[1:3])
    gain_part = jnp.concatenate([gain_one, gain_two], axis=0)
    gain_cols = jnp.pad(gain_part.T, ((0, 0), (0, LANES - 2)))
    parts_width = qkv_width + q_width + LANES
    by_cols = pl.BlockSpec((local_rows, ROWS), lambda i: (0, i))
    attn_parts = pl.pallas_call(
        attn_grads_kernel,
        grid=(width // ROWS,),
        in_specs=[
            pl.BlockSpec(memory_space=pltpu.SMEM),
            pl.BlockSpec((ROWS, rows_all), lambda i: (i, 0)),
            whole((rows_all, qkv_width)),
            by_cols,
            by_cols,
            whole((rows_all, q_width)),
            pl.BlockSpec((ROWS, LANES), lambda i: (i, 0)),
        ],
        out_specs=pl.BlockSpec((ROWS, parts_width), lambda i: (i, 0)),
        out_shape=jax.ShapeDtypeStruct((width, parts_width), BF16),
        compiler_params=pltpu.CompilerParams(vmem_limit_bytes=32 * MIB),
        cost_estimate=pl.CostEstimate(
            flops=2 * rows_all * width * parts_width, bytes_accessed=11 * MIB, transcendentals=0
        ),
        name="attn_grads",
    )(here, normed_one_t, d_qkv, grad_attn, grad_attn_other, o_own, gain_cols)
    attn_grads = lax.psum_scatter(attn_parts, "fsdp", scatter_dimension=0, tiled=True).astype(F32)

    gain_grads = attn_grads[:, qkv_width + q_width :][:, :2].T
    gain_grads = gain_grads + swap(gain_grads)
    grad_one_other = advance(grad_one_other, sums)
    hidden_parts[-1], grad_one_other = lax.optimization_barrier((hidden_parts[-1], grad_one_other))
    moe = run_output(hidden_parts, held_parts, firsts, rows_all, width)
    totals = []
    for part in sums:
        if isinstance(part, PieceSum):
            while part.stage < stages:
                part.send(part.ready())
            part = part.total
        totals.append(part.astype(F32))
    expert_grads = jnp.concatenate(totals, axis=1)
    moe_own = lax.dynamic_slice_in_dim(moe, mine_at, local_rows).astype(F32)
    moe_other = swap(lax.dynamic_slice_in_dim(moe, other_at, local_rows)).astype(F32)
    middle_own = lax.dynamic_slice_in_dim(middle, mine_at, local_rows)
    layer_out = (middle_own + BRANCH_SCALE * (moe_own + moe_other)).astype(BF16)
    grad_one_own = grad_one.astype(F32) + grad_one_other.astype(F32)

    inputs = tokens.astype(F32)
    scale_one = lax.rsqrt(jnp.mean(inputs * inputs, axis=1, keepdims=True) + EPSILON)
    unit_one = inputs * scale_one
    scaled_one = grad_one_own * gain_rows[0:1]
    grad_tokens = (
        grad_middle
        + scale_one
        * (scaled_one - unit_one * jnp.mean(scaled_one * unit_one, axis=1, keepdims=True))
    ).astype(BF16)
    return (
        layer_out,
        grad_tokens,
        attn_grads[:, :q_width],
        attn_grads[:, q_width : q_width + kv_width],
        attn_grads[:, q_width + kv_width : qkv_width],
        attn_grads[:, qkv_width : qkv_width + q_width],
        gain_grads,
        expert_grads[0],
        expert_grads[1],
        expert_grads[2],
    )


def solution(mesh):
    in_specs = (
        P(("fsdp", "tp"), None),
        P("fsdp", None),
        P("fsdp", None),
        P("fsdp", None),
        P("fsdp", "tp"),
        P("fsdp", "tp"),
        P("fsdp", "tp"),
        P("fsdp", "tp"),
        P(None, "fsdp"),
        P(None, "fsdp", "tp"),
        P(None, "fsdp", "tp"),
        P(None, "fsdp", "tp"),
        P(("fsdp", "tp"), None),
    )
    out_specs = (
        P(("fsdp", "tp"), None),
        P(("fsdp", "tp"), None),
        P("fsdp", "tp"),
        P("fsdp", "tp"),
        P("fsdp", "tp"),
        P("fsdp", "tp"),
        P(None, "fsdp"),
        P(None, "fsdp", "tp"),
        P(None, "fsdp", "tp"),
        P(None, "fsdp", "tp"),
    )
    return jax.shard_map(
        per_device, mesh=mesh, in_specs=in_specs, out_specs=out_specs, check_vma=False
    )
```

```python
import functools

import jax
import jax.numpy as jnp
from jax import lax
from jax.experimental import pallas as pl
from jax.experimental.pallas import tpu as pltpu
from jax.sharding import PartitionSpec as P

HEAD_DIM = 64
EXPERTS = 16
MAXLEN = 512
EPSILON = 1e-06
BRANCH_SCALE = 0.22
ROPE_BASE = 10000.0
ROWS = 256
LANES = 128
GATHERED = (12, 4)
SPLIT = (4, 4, 4, 4)
PERMUTED = (True, True, True, True)
DIRECT_MAX = 16
MIB = 1 << 20
BF16 = jnp.bfloat16
F32 = jnp.float32


def dot_nn(left, right):
    return lax.dot_general(left, right, (((1,), (0,)), ((), ())), preferred_element_type=F32)


def dot_nt(left, right):
    return lax.dot_general(left, right, (((1,), (1,)), ((), ())), preferred_element_type=F32)


def dot_tn(left, right):
    return lax.dot_general(left, right, (((0,), (0,)), ((), ())), preferred_element_type=F32)


def seq_layout(lengths, row_total):
    places = jnp.arange(row_total, dtype=jnp.int32)
    ends = jnp.cumsum(lengths)
    starts = ends - lengths
    segment = jnp.sum((places[:, None] >= ends[None, :]).astype(jnp.int32), axis=1)
    chosen = segment[:, None] == jnp.arange(lengths.shape[0], dtype=jnp.int32)[None, :]
    opening = jnp.sum(jnp.where(chosen, starts[None, :], 0), axis=1)
    return (opening, places - opening)


def rotary_tables(position, head_size):
    halfway = head_size // 2
    ladder = jnp.arange(halfway, dtype=F32)
    inverse = jnp.exp(ladder * (-2.0 * jnp.log(ROPE_BASE) / head_size))
    angles = position.astype(F32)[:, None] * inverse[None, :]
    cos_half, sine_half = (jnp.cos(angles), jnp.sin(angles))
    copies = LANES // head_size
    return (
        jnp.concatenate([cos_half, cos_half] * copies, axis=1),
        jnp.concatenate([-sine_half, sine_half] * copies, axis=1),
    )


def rotate_lanes(values, cos_rows, sine_rows):
    lane = lax.broadcasted_iota(jnp.int32, cos_rows.shape, 1)
    first = lane % HEAD_DIM < HEAD_DIM // 2
    parts = []
    for at in range(0, values.shape[1], LANES):
        part = values[:, at : at + LANES]
        partner = jnp.where(
            first,
            pltpu.roll(part, LANES - HEAD_DIM // 2, 1),
            pltpu.roll(part, HEAD_DIM // 2, 1),
        )
        parts.append(part * cos_rows + partner * sine_rows)
    return jnp.concatenate(parts, axis=1)


def key_window(block):
    low = max(0, block * ROWS - ((MAXLEN - 1 + ROWS - 1) // ROWS) * ROWS)
    return (low, (block + 1) * ROWS)


def allowed_pairs(opening_rows, block, low, high):
    shape = (ROWS, high - low)
    query_at = block * ROWS + lax.broadcasted_iota(jnp.int32, shape, 0)
    key_at = low + lax.broadcasted_iota(jnp.int32, shape, 1)
    return (key_at <= query_at) & (key_at >= opening_rows)


def attend_kernel(
    q_width,
    x_ref,
    gain_ref,
    w_ref,
    cos_ref,
    sine_ref,
    opening_ref,
    at_ref,
    q_ref,
    k_ref,
    v_ref,
    o_ref,
    lse_ref,
    gain_rows_ref,
    lse_cols,
):
    rows_all = x_ref.shape[0]
    gain_rows_ref[...] = gain_ref[...].astype(F32).T[: gain_rows_ref.shape[0], :]
    kv_width = k_ref.shape[1]
    kv_heads = kv_width // HEAD_DIM
    group = q_width // kv_width
    scale = HEAD_DIM ** (-0.5)
    for block in range(rows_all // ROWS):
        at = pl.ds(block * ROWS, ROWS)
        x = x_ref[at, :].astype(F32)
        r1 = lax.rsqrt(jnp.mean(x * x, axis=1, keepdims=True) + EPSILON)
        a = (x * r1 * gain_rows_ref[0:1, :]).astype(BF16)
        at_ref[:, at] = a.T
        qkv = dot_nn(a, w_ref[...])
        turned = rotate_lanes(
            qkv[:, : q_width + kv_width], cos_ref[at, :], sine_ref[at, :]
        ).astype(BF16)
        q_ref[at, :] = turned[:, :q_width]
        k_ref[at, :] = turned[:, q_width:]
        v_ref[at, :] = qkv[:, q_width + kv_width :].astype(BF16)
    lane = lax.broadcasted_iota(jnp.int32, (ROWS, LANES), 1)
    for block in range(rows_all // ROWS):
        at = pl.ds(block * ROWS, ROWS)
        low, high = key_window(block)
        keep = allowed_pairs(opening_ref[at, :], block, low, high)
        lse = jnp.zeros((ROWS, LANES), F32)
        outs = []
        for j in range(kv_heads):
            head = slice(j * HEAD_DIM, (j + 1) * HEAD_DIM)
            keys = k_ref[low:high, head]
            vals = v_ref[low:high, head]
            for g in range(group):
                h = j * group + g
                s = dot_nt(q_ref[at, h * HEAD_DIM : (h + 1) * HEAD_DIM], keys) * scale
                s = jnp.where(keep, s, -1e30)
                peak = jnp.max(s, axis=1, keepdims=True)
                p = jnp.exp(s - peak)
                total = jnp.sum(p, axis=1, keepdims=True)
                outs.append((dot_nn(p.astype(BF16), vals) / total).astype(BF16))
                lse = jnp.where(lane == h, peak + jnp.log(total), lse)
        o_ref[at, :] = jnp.concatenate(outs, axis=1)
        lse_cols[at, :] = lse
    lse_ref[...] = lse_cols[...].T[: lse_ref.shape[0], :]


def attend_back_kernel(
    here_ref,
    q_ref,
    k_ref,
    v_ref,
    go_own_ref,
    go_other_ref,
    lse_ref,
    cos_ref,
    sine_ref,
    opening_ref,
    x_ref,
    w_ref,
    d_ref,
    da_own_ref,
    da_send_ref,
    gain_ref,
    dk_acc,
    dv_acc,
    dq_acc,
    go_ref,
):
    here = here_ref[0]
    local_rows = go_own_ref.shape[0]
    go_ref[pl.ds(pl.multiple_of(here * local_rows, local_rows), local_rows), :] = go_own_ref[...]
    go_ref[pl.ds(pl.multiple_of((1 - here) * local_rows, local_rows), local_rows), :] = (
        go_other_ref[...]
    )
    rows_all, q_width = q_ref.shape
    kv_width = k_ref.shape[1]
    kv_heads = kv_width // HEAD_DIM
    group = q_width // kv_width
    scale = HEAD_DIM ** (-0.5)
    blocks = rows_all // ROWS
    dk_acc[...] = jnp.zeros_like(dk_acc)
    dv_acc[...] = jnp.zeros_like(dv_acc)
    for block in range(blocks):
        at = pl.ds(block * ROWS, ROWS)
        low, high = key_window(block)
        shape = (high - low, ROWS)
        query_at = block * ROWS + lax.broadcasted_iota(jnp.int32, shape, 1)
        key_at = low + lax.broadcasted_iota(jnp.int32, shape, 0)
        keep = (key_at <= query_at) & (key_at >= opening_ref[:, at])
        for j in range(kv_heads):
            head = slice(j * HEAD_DIM, (j + 1) * HEAD_DIM)
            keys = k_ref[low:high, head]
            vals = v_ref[low:high, head]
            dk = jnp.zeros((high - low, HEAD_DIM), F32)
            dv = jnp.zeros((high - low, HEAD_DIM), F32)
            for g in range(group):
                h = j * group + g
                mine = slice(h * HEAD_DIM, (h + 1) * HEAD_DIM)
                q = q_ref[at, mine]
                go = go_ref[at, mine]
                s = dot_nt(keys, q) * scale
                p = jnp.where(keep, jnp.exp(s - lse_ref[h : h + 1, at]), 0.0)
                dp = dot_nt(vals, go)
                inner = jnp.sum(p * dp, axis=0, keepdims=True)
                ds = (p * (dp - inner)).astype(BF16)
                dq_acc[at, mine] = dot_tn(ds, keys) * scale
                dk = dk + dot_nn(ds, q)
                dv = dv + dot_nn(p.astype(BF16), go)
            dk_acc[low:high, head] += dk * scale
            dv_acc[low:high, head] += dv
    gain = jnp.zeros((1, x_ref.shape[1]), F32)
    for block in range(blocks):
        at = pl.ds(block * ROWS, ROWS)
        turned = jnp.concatenate([dq_acc[at, :], dk_acc[at, :]], axis=1)
        back = rotate_lanes(turned, cos_ref[at, :], -sine_ref[at, :])
        d = jnp.concatenate([back, dv_acc[at, :]], axis=1).astype(BF16)
        d_ref[at, :] = d
        da = dot_nt(d, w_ref[...])
        half, inside = divmod(block * ROWS, local_rows)
        da_rows = da.astype(BF16)

        @pl.when(here == half)
        def _():
            da_own_ref[inside : inside + ROWS, :] = da_rows

        @pl.when(here != half)
        def _():
            da_send_ref[inside : inside + ROWS, :] = da_rows

        x = x_ref[at, :].astype(F32)
        r1 = lax.rsqrt(jnp.mean(x * x, axis=1, keepdims=True) + EPSILON)
        gain = gain + jnp.sum(da * (x * r1), axis=0, keepdims=True)
    gain_ref[...] = gain


def attn_grads_kernel(here_ref, at_ref, d_ref, own_ref, other_ref, o_ref, gain_ref, parts_ref):
    local_rows = own_ref.shape[0]
    mine = pl.ds(pl.multiple_of(here_ref[0] * local_rows, local_rows), local_rows)
    others = pl.ds(pl.multiple_of((1 - here_ref[0]) * local_rows, local_rows), local_rows)
    qkv_width, q_width = d_ref.shape[1], o_ref.shape[1]
    parts_ref[:, :qkv_width] = dot_nn(at_ref[...], d_ref[...]).astype(BF16)
    out_grad = dot_tn(own_ref[...], o_ref[mine, :]) + dot_tn(other_ref[...], o_ref[others, :])
    parts_ref[:, qkv_width : qkv_width + q_width] = out_grad.astype(BF16)
    parts_ref[:, qkv_width + q_width :] = gain_ref[...].astype(BF16)


def middle_back_kernel(
    here_ref,
    db_ref,
    got_ref,
    x1_ref,
    dy_ref,
    gain_ref,
    w_own_ref,
    w_other_ref,
    dx1_ref,
    attn_ref,
    send_ref,
    own_ref,
    gain_grad_ref,
):
    db = db_ref[...] + got_ref[...].astype(F32)
    x1 = x1_ref[...]
    r2 = lax.rsqrt(jnp.mean(x1 * x1, axis=1, keepdims=True) + EPSILON)
    u2 = x1 * r2
    e2 = db * gain_ref[1:2, :]
    dx1 = dy_ref[...].astype(F32) + r2 * (e2 - u2 * jnp.mean(e2 * u2, axis=1, keepdims=True))
    dx1_ref[...] = dx1
    attn = (BRANCH_SCALE * dx1).astype(BF16)
    attn_ref[...] = attn
    send_ref[...] = dot_nn(attn, w_other_ref[...]).astype(BF16)
    own_ref[...] = dot_nn(attn, w_own_ref[...]).astype(BF16)
    gain_grad = jnp.sum(db * u2, axis=0, keepdims=True)

    @pl.when(pl.program_id(0) == 0)
    def _():
        gain_grad_ref[...] = gain_grad

    @pl.when(pl.program_id(0) > 0)
    def _():
        gain_grad_ref[...] += gain_grad


def middle_kernel(x_ref, own_ref, other_ref, w_own_ref, w_other_ref, gain_ref, x1_ref, b_ref, bt_ref):
    attn = dot_nt(own_ref[...], w_own_ref[...]) + dot_nt(other_ref[...], w_other_ref[...])
    x1 = x_ref[...].astype(F32) + BRANCH_SCALE * attn
    x1_ref[...] = x1
    r2 = lax.rsqrt(jnp.mean(x1 * x1, axis=1, keepdims=True) + EPSILON)
    b = (x1 * r2 * gain_ref[1:2, :]).astype(BF16)
    b_ref[...] = b
    bt_ref[...] = b.T


def piece_of(d):
    if d == 0:
        return 0, 0
    n = (d & -d).bit_length()
    return n, d >> n


def experts_kernel(
    started,
    last,
    stages,
    place_ref,
    b_ref,
    bt_ref,
    dy_ref,
    dyt_ref,
    gates_ref,
    w_ref,
    db_in,
    *refs,
):
    g_refs, refs = refs[: stages + 1], refs[stages + 1 :]
    h_ref, db_ref, refs = refs[0], refs[1], refs[2:]
    g_scr = refs[-1]
    step = pl.program_id(0)
    rows_all, width = b_ref.shape

    @pl.when(step == 0)
    def _():
        db_ref[...] = db_in[...] if started else jnp.zeros_like(db_ref)

    hidden = w_ref.shape[-1]
    gate_w, up_w, down_w = [w_ref[:, kind, 0].reshape(width, hidden) for kind in range(3)]
    lane = lax.broadcasted_iota(jnp.int32, (ROWS, gates_ref.shape[1]), 1)
    weighted, gate_grads, up_grads = [], [], []
    for block in range(rows_all // ROWS):
        at = pl.ds(block * ROWS, ROWS)
        b = b_ref[at, :]
        route = jnp.sum(
            jnp.where(lane == place_ref[1] + step, gates_ref[at, :], 0.0), axis=1, keepdims=True
        )
        gate = dot_nn(b, gate_w)
        up = dot_nn(b, up_w)
        back = dot_nn(dy_ref[at, :], down_w) * (route * BRANCH_SCALE)
        sig = jax.nn.sigmoid(gate)
        silu = gate * sig
        h = (silu * up * route).astype(BF16)
        dg = (back * up * sig * (1.0 + gate * (1.0 - sig))).astype(BF16)
        du = (back * silu).astype(BF16)
        h_ref[at, :] = h
        db_ref[at, :] += dot_nt(dg, gate_w) + dot_nt(du, up_w)
        weighted.append(h)
        gate_grads.append(dg)
        up_grads.append(du)
    for kind, left_ref, right, scale in (
        (0, bt_ref, gate_grads, None),
        (1, bt_ref, up_grads, None),
        (2, dyt_ref, weighted, BRANCH_SCALE),
    ):
        grad = dot_nn(left_ref[...], jnp.concatenate(right, axis=0))
        if scale is not None:
            grad = grad * scale
        g_scr[kind] = grad.astype(BF16).reshape(g_scr.shape[1:])
    for d in range(g_scr.shape[1]):
        n, at = piece_of(d) if stages else (0, d)
        source = d ^ place_ref[0] if stages else d
        for kind in range(3):
            g_refs[n][at, kind, 0] = g_scr[kind, source]

    if last:

        @pl.when(step == pl.num_programs(0) - 1)
        def _():
            send_ref = refs[0]
            rows = send_ref.shape[0]
            start = pl.multiple_of(place_ref[2], rows)
            send_ref[...] = db_ref[pl.ds(start, rows), :].astype(BF16)


def output_kernel(counts, *refs):
    chunks = len(counts)
    h_refs, w_refs, (moe_ref, acc) = refs[:chunks], refs[chunks : 2 * chunks], refs[2 * chunks :]
    step = pl.program_id(0)
    width, hidden = acc.shape[1], w_refs[0].shape[-1]

    @pl.when(step == 0)
    def _():
        acc[...] = jnp.zeros_like(acc)

    def add(held):
        acc[...] += sum(
            dot_nt(h_refs[n][...], w_refs[n][:, 0, 0].reshape(width, hidden)) for n in held
        )

    limits = sorted(set(counts))
    for low, high in zip([0] + limits, limits):
        held = [n for n in range(chunks) if counts[n] >= high]
        pl.when((step >= low) & (step < high))(functools.partial(add, held))

    @pl.when(step == pl.num_programs(0) - 1)
    def _():
        moe_ref[...] = acc[...].astype(BF16)


def whole(shape):
    return pl.BlockSpec(shape, lambda *_: (0,) * len(shape), pipeline_mode=pl.Buffered(1))


def run_experts(
    place, b, bt, dy, dyt, gates, weights, first, count, parts, stages, carried, last
):
    rows_all, width = b.shape
    shards, kinds, _, per_shard, hidden = weights.shape
    out_rows = width // parts
    sizes = [1] + [1 << (stages - n) for n in range(1, stages + 1)] if stages else [parts]
    local_rows = rows_all // 2
    started = carried is not None
    if not started:
        carried = jnp.zeros((8, LANES), F32)
    results = pl.pallas_call(
        functools.partial(experts_kernel, started, last, stages),
        grid_spec=pltpu.PrefetchScalarGridSpec(
            num_scalar_prefetch=1,
            grid=(count,),
            in_specs=[whole(t.shape) for t in (b, bt, dy, dyt, gates)]
            + [
                pl.BlockSpec(
                    (shards, kinds, 1, per_shard, hidden),
                    lambda e, place: (0, 0, first + e, 0, 0),
                ),
                whole(carried.shape),
            ],
            out_specs=[
                pl.BlockSpec(
                    (size, kinds, 1, out_rows, hidden), lambda e, place: (0, 0, e, 0, 0)
                )
                for size in sizes
            ]
            + [
                pl.BlockSpec((rows_all, hidden), lambda e, place: (0, e)),
                whole((rows_all, width)),
            ]
            + [whole((local_rows, width))] * last,
            scratch_shapes=[pltpu.VMEM((kinds, parts, out_rows, hidden), BF16)],
        ),
        out_shape=[
            jax.ShapeDtypeStruct((size, kinds, count, out_rows, hidden), BF16) for size in sizes
        ]
        + [
            jax.ShapeDtypeStruct((rows_all, count * hidden), BF16),
            jax.ShapeDtypeStruct((rows_all, width), F32),
        ]
        + [jax.ShapeDtypeStruct((local_rows, width), BF16)] * last,
        compiler_params=pltpu.CompilerParams(vmem_limit_bytes=48 * MIB),
        cost_estimate=pl.CostEstimate(
            flops=8 * 2 * rows_all * width * hidden * count,
            bytes_accessed=4 * kinds * count * width * hidden + 18 * MIB,
            transcendentals=0,
        ),
        name="experts",
    )(place, b, bt, dy, dyt, gates, weights, carried)
    pieces = len(sizes)
    return results[:pieces], results[pieces], results[pieces + 1], results[pieces + 2 :]


def run_output(hidden_parts, weight_parts, firsts, rows_all, width):
    shards, _, _, per_shard, hidden = weight_parts[0].shape
    counts = [h.shape[1] // hidden for h in hidden_parts]

    def hidden_spec(count):
        return pl.BlockSpec((rows_all, hidden), lambda e: (0, jnp.minimum(e, count - 1)))

    def weight_spec(first, count):
        return pl.BlockSpec(
            (shards, 1, 1, per_shard, hidden),
            lambda e: (0, 2, first + jnp.minimum(e, count - 1), 0, 0),
        )

    return pl.pallas_call(
        functools.partial(output_kernel, counts),
        grid=(max(counts),),
        in_specs=[hidden_spec(count) for count in counts]
        + [weight_spec(first, count) for first, count in zip(firsts, counts)],
        out_specs=whole((rows_all, width)),
        out_shape=jax.ShapeDtypeStruct((rows_all, width), BF16),
        scratch_shapes=[pltpu.VMEM((rows_all, width), F32)],
        compiler_params=pltpu.CompilerParams(vmem_limit_bytes=40 * MIB),
        cost_estimate=pl.CostEstimate(
            flops=2 * rows_all * width * hidden * sum(counts),
            bytes_accessed=18 * MIB,
            transcendentals=0,
        ),
        name="expert_output",
    )(*hidden_parts, *weight_parts)


class PieceSum:
    def __init__(self, pieces, shards):
        self.shards = shards
        self.stages = len(pieces) - 1
        self.own, self.rest = pieces[0], pieces[1:]
        self.stage = 0
        self.got = self.swap(self.rest[0])

    def swap(self, values):
        bit = 1 << self.stage
        return lax.ppermute(values, "fsdp", [(s, s ^ bit) for s in range(self.shards)])

    def ready(self):
        if self.stage == self.stages - 1:
            return [self.own.astype(F32) + self.got[:1].astype(F32)]
        left = [self.own + self.got[:1]]
        for n, piece in enumerate(self.rest[self.stage + 1 :]):
            left.append(piece + self.got[1 << n :: 2 << n])
        return left

    def send(self, values):
        if self.stage == self.stages - 1:
            self.total = values[0][0]
            self.stage += 1
            return
        self.stage += 1
        self.own = values[0]
        self.rest = [None] * self.stage + values[1:]
        self.got = self.swap(self.rest[self.stage])


def per_device(
    tokens,
    seq_lens,
    routes,
    route_gates,
    query_weight,
    key_matrix,
    value_matrix,
    out_weight,
    norm_gains,
    gate_weight,
    up_weight,
    down_weight,
    cotangent,
):
    local_rows, width = tokens.shape
    rows_all = local_rows * 2
    shards = lax.axis_size("fsdp")
    per_shard = width // shards
    q_width = query_weight.shape[1]
    kv_width = key_matrix.shape[1]
    qkv_width = q_width + 2 * kv_width
    place = lax.axis_index("tp")
    mine_at = place * local_rows
    other_at = (1 - place) * local_rows

    def swap(values):
        return lax.ppermute(values, "tp", [(0, 1), (1, 0)])

    def both(own, other):
        return lax.dynamic_update_slice_in_dim(
            jnp.concatenate([own, own], axis=0), other, other_at, axis=0
        )

    attn_local = jnp.concatenate(
        [
            query_weight,
            key_matrix,
            value_matrix,
            out_weight,
            jnp.pad(norm_gains.T, ((0, 0), (0, LANES - 2))),
        ],
        axis=1,
    )
    attn_w = lax.all_gather(attn_local, "fsdp", axis=0, tiled=True)
    hidden_width = gate_weight.shape[-1]
    expert_w, expert_at = [], []
    start = 0
    for count in GATHERED:
        part = jnp.concatenate(
            [
                w[start : start + count].reshape(-1, hidden_width)
                for w in (gate_weight, up_weight, down_weight)
            ]
        )
        part = lax.all_gather(part, "fsdp", axis=0, tiled=True)
        part = part.reshape(shards, 3, count, per_shard, hidden_width)
        if per_shard % 16 != 0:
            part = part.transpose(1, 2, 0, 3, 4).reshape(1, 3, count, width, hidden_width)
        expert_w.append(part)
        expert_at += [(len(expert_w) - 1, at) for at in range(count)]
        start += count
    stages = shards.bit_length() - 1
    whole_tiles = per_shard % 16 == 0
    direct = 2 <= shards <= DIRECT_MAX and 1 << stages == shards and whole_tiles
    index = lax.axis_index("fsdp") if direct else 0

    x_full = both(tokens, swap(tokens))
    dy_full = both(cotangent, swap(cotangent))
    dy_t = dy_full.T
    opening, position = seq_layout(seq_lens[0], rows_all)
    cos_table, sine_table = rotary_tables(position, HEAD_DIM)
    gates = jnp.sum(
        jnp.where(
            routes[:, :, None] == jnp.arange(LANES, dtype=jnp.int32)[None, None, :],
            route_gates[:, :, None],
            0.0,
        ),
        axis=1,
    )

    out_own, x_full = lax.optimization_barrier(
        (attn_w[:, qkv_width : qkv_width + q_width], x_full)
    )
    out_other = swap(out_own)
    heads = q_width // HEAD_DIM
    rows_of = lambda n, t: jax.ShapeDtypeStruct((rows_all, n), t)
    normed_one_t, q_rows, k_rows, v_rows, o_own, lse, gain_rows = pl.pallas_call(
        functools.partial(attend_kernel, q_width),
        grid=(1,),
        in_specs=[
            whole((rows_all, width)),
            pl.BlockSpec(
                (width, LANES),
                lambda i: (0, (qkv_width + q_width) // LANES),
                pipeline_mode=pl.Buffered(1),
            ),
            whole((width, qkv_width)),
            whole((rows_all, LANES)),
            whole((rows_all, LANES)),
            whole((rows_all, 1)),
        ],
        out_specs=[
            whole((width, rows_all)),
            whole((rows_all, q_width)),
            whole((rows_all, kv_width)),
            whole((rows_all, kv_width)),
            whole((rows_all, q_width)),
            whole((heads, rows_all)),
            whole((8, width)),
        ],
        out_shape=[
            jax.ShapeDtypeStruct((width, rows_all), BF16),
            rows_of(q_width, BF16),
            rows_of(kv_width, BF16),
            rows_of(kv_width, BF16),
            rows_of(q_width, BF16),
            jax.ShapeDtypeStruct((heads, rows_all), F32),
            jax.ShapeDtypeStruct((8, width), F32),
        ],
        scratch_shapes=[pltpu.VMEM((rows_all, LANES), F32)],
        compiler_params=pltpu.CompilerParams(vmem_limit_bytes=48 * MIB),
        cost_estimate=pl.CostEstimate(
            flops=8 * rows_all * width * qkv_width, bytes_accessed=12 * MIB, transcendentals=0
        ),
        name="attend",
    )(x_full, attn_w, attn_w, cos_table, sine_table, opening[:, None])

    o_other = swap(o_own)
    steps = rows_all // ROWS
    by_rows = lambda n: pl.BlockSpec((ROWS, n), lambda i: (i, 0))
    first_out = qkv_width // q_width
    middle, normed_two, normed_two_t = pl.pallas_call(
        middle_kernel,
        grid=(steps,),
        in_specs=[
            by_rows(width),
            by_rows(q_width),
            by_rows(q_width),
            pl.BlockSpec((width, q_width), lambda i: (0, first_out)),
            pl.BlockSpec((width, q_width), lambda i: (0, 0)),
            pl.BlockSpec((8, width), lambda i: (0, 0)),
        ],
        out_specs=[
            by_rows(width),
            by_rows(width),
            pl.BlockSpec((width, ROWS), lambda i: (0, i)),
        ],
        out_shape=[
            rows_of(width, F32),
            rows_of(width, BF16),
            jax.ShapeDtypeStruct((width, rows_all), BF16),
        ],
        compiler_params=pltpu.CompilerParams(vmem_limit_bytes=32 * MIB),
        cost_estimate=pl.CostEstimate(
            flops=4 * rows_all * width * q_width, bytes_accessed=14 * MIB, transcendentals=0
        ),
        name="middle",
    )(x_full, o_own, o_other, attn_w, out_other, gain_rows)

    def advance(anchor, parts):
        parts = [part for part in parts if isinstance(part, PieceSum)]
        if not parts:
            return anchor
        parts = [part for part in parts if part.stage < part.stages]
        if not parts:
            return anchor
        values = [part.ready() for part in parts]
        anchor, values = lax.optimization_barrier((anchor, values))
        for part, value in zip(parts, values):
            part.send(value)
        return anchor

    grad_two = None
    sums, hidden_parts, held_parts, firsts = [], [], [], []
    start = 0
    for count in SPLIT:
        if len(sums) >= 2:
            grad_two = advance(grad_two, sums[:-1])
        permuted = direct and PERMUTED[len(sums)]
        held, first = expert_at[start]
        where = jnp.stack([index, start, other_at]).astype(jnp.int32)
        grads, hidden, grad_two, sent = run_experts(
            where,
            normed_two,
            normed_two_t,
            dy_full,
            dy_t,
            gates,
            expert_w[held],
            first,
            count,
            shards if whole_tiles else 1,
            stages if permuted else 0,
            grad_two,
            start + count == EXPERTS,
        )
        hidden_parts.append(hidden)
        held_parts.append(expert_w[held])
        firsts.append(first)
        if permuted:
            sums.append(PieceSum(grads, shards))
        else:
            grads = grads[0]
            if not whole_tiles:
                grads = grads.reshape(3, count, shards, per_shard, -1).transpose(2, 0, 1, 3, 4)
            grads = lax.psum_scatter(
                grads.reshape(-1, hidden_width), "fsdp", scatter_dimension=0, tiled=True
            )
            sums.append(grads.reshape(3, count, per_shard, hidden_width))
        start += count

    grad_two_other = swap(sent[0])
    grad_two_other = advance(grad_two_other, sums[2:])
    here = place.astype(jnp.int32)[None]
    steps = local_rows // ROWS
    own_block = lambda i, here: (here[0] * steps + i, 0)
    local_block = lambda i, here: (i, 0)
    grad_middle, grad_attn, go_send, go_own, gain_two = pl.pallas_call(
        middle_back_kernel,
        grid_spec=pltpu.PrefetchScalarGridSpec(
            num_scalar_prefetch=1,
            grid=(steps,),
            in_specs=[
                pl.BlockSpec((ROWS, width), own_block),
                pl.BlockSpec((ROWS, width), local_block),
                pl.BlockSpec((ROWS, width), own_block),
                pl.BlockSpec((ROWS, width), local_block),
                whole((8, width)),
                whole((width, q_width)),
                whole((width, q_width)),
            ],
            out_specs=[
                pl.BlockSpec((ROWS, width), local_block),
                pl.BlockSpec((ROWS, width), local_block),
                pl.BlockSpec((ROWS, q_width), local_block),
                pl.BlockSpec((ROWS, q_width), local_block),
                whole((1, width)),
            ],
        ),
        out_shape=[
            jax.ShapeDtypeStruct((local_rows, width), F32),
            jax.ShapeDtypeStruct((local_rows, width), BF16),
            jax.ShapeDtypeStruct((local_rows, q_width), BF16),
            jax.ShapeDtypeStruct((local_rows, q_width), BF16),
            jax.ShapeDtypeStruct((1, width), F32),
        ],
        compiler_params=pltpu.CompilerParams(vmem_limit_bytes=32 * MIB),
        cost_estimate=pl.CostEstimate(
            flops=4 * local_rows * width * q_width, bytes_accessed=12 * MIB, transcendentals=0
        ),
        name="middle_back",
    )(here, grad_two, grad_two_other, middle, cotangent, gain_rows, out_own, out_other)
    go_other = swap(go_send)
    go_other, attn_send = lax.optimization_barrier((go_other, grad_attn))
    grad_attn_other = swap(attn_send)
    go_other = advance(go_other, sums[:2])

    d_qkv, grad_one, grad_one_send, gain_one = pl.pallas_call(
        attend_back_kernel,
        grid=(1,),
        in_specs=[
            pl.BlockSpec(memory_space=pltpu.SMEM),
            whole((rows_all, q_width)),
            whole((rows_all, kv_width)),
            whole((rows_all, kv_width)),
            whole((local_rows, q_width)),
            whole((local_rows, q_width)),
            whole((heads, rows_all)),
            whole((rows_all, LANES)),
            whole((rows_all, LANES)),
            whole((1, rows_all)),
            whole((rows_all, width)),
            whole((width, qkv_width)),
        ],
        out_specs=[
            whole((rows_all, qkv_width)),
            whole((local_rows, width)),
            whole((local_rows, width)),
            whole((1, width)),
        ],
        out_shape=[
            rows_of(qkv_width, BF16),
            jax.ShapeDtypeStruct((local_rows, width), BF16),
            jax.ShapeDtypeStruct((local_rows, width), BF16),
            jax.ShapeDtypeStruct((1, width), F32),
        ],
        scratch_shapes=[
            pltpu.VMEM((rows_all, kv_width), F32),
            pltpu.VMEM((rows_all, kv_width), F32),
            pltpu.VMEM((rows_all, q_width), F32),
            pltpu.VMEM((rows_all, q_width), BF16),
        ],
        compiler_params=pltpu.CompilerParams(vmem_limit_bytes=48 * MIB),
        cost_estimate=pl.CostEstimate(
            flops=16 * rows_all * width * qkv_width, bytes_accessed=12 * MIB, transcendentals=0
        ),
        name="attend_back",
    )(
        here,
        q_rows,
        k_rows,
        v_rows,
        go_own,
        go_other,
        lse,
        cos_table,
        sine_table,
        opening[None, :],
        x_full,
        attn_w,
    )

    grad_one_other = swap(grad_one_send)
    d_qkv = advance(d_qkv, sums[:3])
    gain_part = jnp.concatenate([gain_one, gain_two], axis=0)
    gain_cols = jnp.pad(gain_part.T, ((0, 0), (0, LANES - 2)))
    parts_width = qkv_width + q_width + LANES
    by_cols = pl.BlockSpec((local_rows, ROWS), lambda i: (0, i))
    attn_parts = pl.pallas_call(
        attn_grads_kernel,
        grid=(width // ROWS,),
        in_specs=[
            pl.BlockSpec(memory_space=pltpu.SMEM),
            pl.BlockSpec((ROWS, rows_all), lambda i: (i, 0)),
            whole((rows_all, qkv_width)),
            by_cols,
            by_cols,
            whole((rows_all, q_width)),
            pl.BlockSpec((ROWS, LANES), lambda i: (i, 0)),
        ],
        out_specs=pl.BlockSpec((ROWS, parts_width), lambda i: (i, 0)),
        out_shape=jax.ShapeDtypeStruct((width, parts_width), BF16),
        compiler_params=pltpu.CompilerParams(vmem_limit_bytes=32 * MIB),
        cost_estimate=pl.CostEstimate(
            flops=2 * rows_all * width * parts_width, bytes_accessed=11 * MIB, transcendentals=0
        ),
        name="attn_grads",
    )(here, normed_one_t, d_qkv, grad_attn, grad_attn_other, o_own, gain_cols)
    attn_grads = lax.psum_scatter(attn_parts, "fsdp", scatter_dimension=0, tiled=True).astype(F32)

    gain_grads = attn_grads[:, qkv_width + q_width :][:, :2].T
    gain_grads = gain_grads + swap(gain_grads)
    hidden_parts[-1], attn_parts = lax.optimization_barrier((hidden_parts[-1], attn_parts))
    moe = run_output(hidden_parts, held_parts, firsts, rows_all, width)
    grad_one_other, moe = lax.optimization_barrier((grad_one_other, moe))
    grad_one_other = advance(grad_one_other, sums[1:])
    totals = []
    for part in sums:
        if isinstance(part, PieceSum):
            while part.stage < stages:
                part.send(part.ready())
            part = part.total
        totals.append(part.astype(F32))
    expert_grads = jnp.concatenate(totals, axis=1)
    moe_own = lax.dynamic_slice_in_dim(moe, mine_at, local_rows).astype(F32)
    moe_other = swap(lax.dynamic_slice_in_dim(moe, other_at, local_rows)).astype(F32)
    middle_own = lax.dynamic_slice_in_dim(middle, mine_at, local_rows)
    layer_out = (middle_own + BRANCH_SCALE * (moe_own + moe_other)).astype(BF16)
    grad_one_own = grad_one.astype(F32) + grad_one_other.astype(F32)

    inputs = tokens.astype(F32)
    scale_one = lax.rsqrt(jnp.mean(inputs * inputs, axis=1, keepdims=True) + EPSILON)
    unit_one = inputs * scale_one
    scaled_one = grad_one_own * gain_rows[0:1]
    grad_tokens = (
        grad_middle
        + scale_one
        * (scaled_one - unit_one * jnp.mean(scaled_one * unit_one, axis=1, keepdims=True))
    ).astype(BF16)
    return (
        layer_out,
        grad_tokens,
        attn_grads[:, :q_width],
        attn_grads[:, q_width : q_width + kv_width],
        attn_grads[:, q_width + kv_width : qkv_width],
        attn_grads[:, qkv_width : qkv_width + q_width],
        gain_grads,
        expert_grads[0],
        expert_grads[1],
        expert_grads[2],
    )


def solution(mesh):
    in_specs = (
        P(("fsdp", "tp"), None),
        P("fsdp", None),
        P("fsdp", None),
        P("fsdp", None),
        P("fsdp", "tp"),
        P("fsdp", "tp"),
        P("fsdp", "tp"),
        P("fsdp", "tp"),
        P(None, "fsdp"),
        P(None, "fsdp", "tp"),
        P(None, "fsdp", "tp"),
        P(None, "fsdp", "tp"),
        P(("fsdp", "tp"), None),
    )
    out_specs = (
        P(("fsdp", "tp"), None),
        P(("fsdp", "tp"), None),
        P("fsdp", "tp"),
        P("fsdp", "tp"),
        P("fsdp", "tp"),
        P("fsdp", "tp"),
        P(None, "fsdp"),
        P(None, "fsdp", "tp"),
        P(None, "fsdp", "tp"),
        P(None, "fsdp", "tp"),
    )
    return jax.shard_map(
        per_device, mesh=mesh, in_specs=in_specs, out_specs=out_specs, check_vma=False
    )
```
